512 devices in a mesh: ens: 8 (over z_hi, y), space: 64 (over x, z_lo, core).
Axes of the slice: x: 4, y: 4, z: 16 (z_hi: 2, z_lo: 8; z = z_hi * 8 + z_lo), core: 2. Of those that a mesh axis runs over, the one named last changes fastest.
Arguments:
- node_states: bfloat16 [8, 8192, 1024], P('ens', 'space'), may hold values from -6 to 6
- query: bfloat16 [8, 8192, 512], P('ens', 'space'), may hold values from -240 to 240
- key: bfloat16 [8, 8192, 512], P('ens', 'space'), may hold values from -6 to 6
- value: bfloat16 [8, 8192, 512], P('ens', 'space'), may hold values from -6 to 6
- out_weight: bfloat16 [512, 1024], replicated, may hold values from -0.25 to 0.25
- dec_weight: bfloat16 [100, 1024], replicated, may hold values from -0.1875 to 0.1875
- target: float32 [100, 65536], P(None, 'space'), may hold values from -6 to 6
- area_weight: float32 [65536], P('space'), may hold values from 0.25 to 2.5
- var_weight: float32 [100], replicated, may hold values from 0.5 to 5
- edges: int32 [3, 65536], P(None, 'space'), may hold values from 0 to 8191, as said below
- edge_weight: float32 [3, 65536], P(None, 'space'), may hold values from 0.1 to 0.6
- windows: int32 [2, 64], P(None, 'space'), may hold values from 0 to 8192, as said below
Outputs:
- grad_states: bfloat16 [8, 8192, 1024], P('ens', 'space')
- grad_query: bfloat16 [8, 8192, 512], P('ens', 'space')
- grad_key: bfloat16 [8, 8192, 512], P('ens', 'space')
- grad_value: bfloat16 [8, 8192, 512], P('ens', 'space')
- grad_wo: float32 [512, 1024], P('space')
- grad_dec: float32 [100, 1024], replicated
The draws below stay inside these ranges and needn't reach their ends.
Inputs may be any that keep to these rules, and one draw needn't show every extreme that they name: The edges of a point among the 1024 points p with p // 1024 = d name nodes from d * 128 - 128 to d * 128 + 2 * 128 - 1; both ends are named in every draw. For the block b of nodes s = b * 128 to s + 127: max(0, s - 128) <= windows[0, b] <= s and s + 128 <= windows[1, b] <= min(8192, s + 256); the outer ends s - 128 and s + 256 are reached by some block in every draw.
All inputs are finite; a program needn't handle non-finite values.
Results may differ from the reference program's by a relative error of at most 0.017.
Values may be sent and summed in bfloat16 or wider, within the bound.
No kernel may reach another device: no remote copies, remote signals or barrier semaphores. Data moves between devices by JAX's collectives and lax.ppermute only.
A program may use at most 64 MiB of HBM per device.

```python
import math
import jax
import jax.numpy as jnp
from jax import lax

D = 1024
V = 100
HEADS = 8
HEAD_DIM = 64
KNB = 3
BLOCK = 128
NODE_DEV = 128
PT_DEV = 1024
ATT = 512
MEMBERS = 8
NODES = 8192
POINTS = 65536
N_SPACE = 64


def query_key_pair(key):
    base_key = jax.random.fold_in(key, 17)
    query_seed, key_seed = jax.random.split(base_key, 2)
    shape_full = (MEMBERS, NODES, ATT)
    queries = jnp.clip(jax.random.normal(query_seed, shape_full, jnp.float32), -6.0, 6.0)
    keys_drawn = jnp.clip(jax.random.normal(key_seed, shape_full, jnp.float32), -6.0, 6.0)
    return (queries, keys_drawn)


def draw_query(key, part):
    return query_key_pair(key)[0].astype(jnp.bfloat16)


def draw_key(key, part):
    return query_key_pair(key)[1].astype(jnp.bfloat16)


def draw_edges(key, part):
    offset_seed, low_seed, high_seed = jax.random.split(jax.random.fold_in(key, 29), 3)
    point_ids = jnp.arange(POINTS)
    band_ids = point_ids // PT_DEV
    base_node = band_ids * NODE_DEV + point_ids % PT_DEV * NODE_DEV // PT_DEV
    offsets = jax.random.randint(offset_seed, (KNB, POINTS), -NODE_DEV, NODE_DEV)
    node_ids = base_node[None, :] + offsets
    low_band = jax.random.randint(low_seed, (), 1, N_SPACE)
    high_band = jax.random.randint(high_seed, (), 0, N_SPACE - 1)
    slot_ids = jnp.arange(KNB)[:, None]
    lowest_spot = (point_ids[None, :] == low_band * PT_DEV) & (slot_ids == 0)
    highest_spot = (point_ids[None, :] == high_band * PT_DEV + PT_DEV - 1) & (slot_ids == 0)
    node_ids = jnp.where(lowest_spot, low_band * NODE_DEV - NODE_DEV, node_ids)
    node_ids = jnp.where(highest_spot, high_band * NODE_DEV + 2 * NODE_DEV - 1, node_ids)
    return jnp.clip(node_ids, 0, NODES - 1).astype(jnp.int32)


def draw_windows(key, part):
    back_seed, ahead_seed, first_seed, last_seed = jax.random.split(jax.random.fold_in(key, 41), 4)
    block_count = NODES // BLOCK
    per_band = NODE_DEV // BLOCK
    block_ids = jnp.arange(block_count)
    reach_back = jax.random.randint(back_seed, (block_count,), NODE_DEV // 4, NODE_DEV + 1)
    reach_ahead = jax.random.randint(ahead_seed, (block_count,), NODE_DEV // 4, NODE_DEV + 1)
    first_pick = jax.random.randint(first_seed, (), 1, N_SPACE) * per_band
    last_pick = jax.random.randint(last_seed, (), 0, N_SPACE - 1) * per_band + per_band - 1
    reach_back = jnp.where(block_ids == first_pick, NODE_DEV, reach_back)
    reach_ahead = jnp.where(block_ids == last_pick, NODE_DEV, reach_ahead)
    block_start = block_ids * BLOCK
    lower_end = jnp.maximum(block_start - reach_back, 0)
    upper_end = jnp.minimum(block_start + BLOCK + reach_ahead, NODES)
    return jnp.stack([lower_end, upper_end]).astype(jnp.int32)


def block_scale(stream_key, dims, pieces, low, largest):
    level, own = 1.0, jax.random.fold_in(stream_key, 6)
    for axis_at, blocks in pieces:
        steps = jnp.exp(jax.random.uniform(jax.random.fold_in(own, axis_at), (blocks,), jnp.float32, low / len(pieces), largest / len(pieces)))
        level = level * jnp.repeat(steps, dims[axis_at] // blocks).reshape([-1 if axis == axis_at else 1 for axis in range(len(dims))])
    return level


def normal_values(rng, dims, deviation, reach, shards=(), kind=jnp.bfloat16):
    loudness = block_scale(rng, dims, shards, -0.22, 0.18) if shards else 1.0
    entries = jax.random.normal(rng, dims, jnp.float32) * deviation * loudness
    return jnp.minimum(jnp.maximum(entries, -reach), reach).astype(kind)


def setup_inputs(seed: int = 0) -> dict:
    streams_of = jax.random.split(jax.random.key(seed), 13)
    node_states = normal_values(streams_of[0], (MEMBERS, NODES, D), 1.0, 6.0, ((0, 8), (1, 64)))
    query = draw_query(jax.random.fold_in(streams_of[12], 71), 0)
    key = draw_key(jax.random.fold_in(streams_of[12], 71), 0)
    value = normal_values(streams_of[3], (MEMBERS, NODES, ATT), 1.0, 6.0, ((0, 8), (1, 64)))
    out_weight = normal_values(streams_of[4], (ATT, D), ATT ** -0.5, 0.25)
    dec_weight = normal_values(streams_of[5], (V, D), D ** -0.5, 0.1875)
    target = normal_values(streams_of[6], (V, POINTS), 1.0, 6.0, ((1, 64),), jnp.float32)
    area_weight = jnp.clip(jnp.exp(math.log(2.5) - 2.3025851 * jax.random.uniform(streams_of[7], (POINTS,), jnp.float32) ** block_scale(streams_of[7], (POINTS,), ((0, 64),), -0.2, 0.2)), 0.25, 2.5)
    var_weight = jnp.clip(jnp.exp(jax.random.uniform(streams_of[8], (V,), jnp.float32, math.log(0.5), math.log(5.0))), 0.5, 5.0)
    edges = draw_edges(jax.random.fold_in(streams_of[12], 71), 0)
    edge_weight = jnp.clip(0.1 + 0.5 * jax.random.uniform(streams_of[10], (KNB, POINTS), jnp.float32) ** block_scale(streams_of[10], (KNB, POINTS), ((1, 64),), -0.2, 0.2), 0.1, 0.6)
    windows = draw_windows(jax.random.fold_in(streams_of[12], 71), 0)
    return dict(node_states=node_states, query=query, key=key, value=value, out_weight=out_weight, dec_weight=dec_weight, target=target, area_weight=area_weight, var_weight=var_weight, edges=edges, edge_weight=edge_weight, windows=windows)


SMOOTH_SQUARE = 0.0625
MASKED_SCORE = -1e+30

def smooth_slope(diff_value):
    return diff_value * lax.rsqrt(diff_value * diff_value + SMOOTH_SQUARE)

def decode(states, edges, edge_weight):
    latent_sum = jnp.zeros((edges.shape[1], states.shape[1]), jnp.float32)
    for edge_slot in range(edges.shape[0]):
        latent_sum = latent_sum + edge_weight[edge_slot][:, None] * jnp.take(states, edges[edge_slot], axis=0).astype(jnp.float32)
    return latent_sum.astype(jnp.bfloat16)

def attention_grads(query, key, value, grad_states, out_weight, windows):
    node_count = query.shape[0]
    key_span = BLOCK + 2 * NODE_DEV
    padding = ((NODE_DEV, NODE_DEV), (0, 0))
    key_pad = jnp.pad(key, padding)
    value_pad = jnp.pad(value, padding)
    grad_out = jnp.dot(grad_states, out_weight.T, preferred_element_type=jnp.float32).astype(jnp.bfloat16)
    score_scale = 1.0 / math.sqrt(HEAD_DIM)

    def one_block(totals, block_index):
        key_grads, value_grads = totals
        first_row = block_index * BLOCK
        query_heads = lax.dynamic_slice_in_dim(query, first_row, BLOCK, 0).astype(jnp.float32).reshape(BLOCK, HEADS, HEAD_DIM)
        key_heads = lax.dynamic_slice_in_dim(key_pad, first_row, key_span, 0).astype(jnp.float32).reshape(key_span, HEADS, HEAD_DIM)
        value_heads = lax.dynamic_slice_in_dim(value_pad, first_row, key_span, 0).astype(jnp.float32).reshape(key_span, HEADS, HEAD_DIM)
        grad_heads = lax.dynamic_slice_in_dim(grad_out, first_row, BLOCK, 0).astype(jnp.float32).reshape(BLOCK, HEADS, HEAD_DIM)
        key_place = first_row - NODE_DEV + jnp.arange(key_span, dtype=jnp.int32)
        inside = (key_place >= windows[0, block_index]) & (key_place < windows[1, block_index])
        scores = jnp.einsum('qhc,khc->hqk', query_heads, key_heads) * score_scale
        scores = jnp.where(inside[None, None, :], scores, MASKED_SCORE)
        row_max = lax.optimization_barrier(jnp.max(scores, axis=-1, keepdims=True))
        exponent = jnp.exp(scores - row_max)
        attn_prob = exponent / lax.optimization_barrier(jnp.sum(exponent, axis=-1, keepdims=True))
        prob_low = lax.optimization_barrier(attn_prob.astype(jnp.bfloat16)).astype(jnp.float32)
        attn_rows = jnp.einsum('hqk,khc->qhc', prob_low, value_heads).reshape(BLOCK, -1).astype(jnp.bfloat16)
        value_term = jnp.einsum('hqk,qhc->khc', prob_low, grad_heads).reshape(key_span, -1)
        grad_prob = jnp.einsum('qhc,khc->hqk', grad_heads, value_heads)
        row_delta = lax.optimization_barrier(jnp.sum(attn_prob * grad_prob, axis=-1, keepdims=True))
        grad_scores = lax.optimization_barrier((attn_prob * (grad_prob - row_delta)).astype(jnp.bfloat16)).astype(jnp.float32)
        query_rows = (jnp.einsum('hqk,khc->qhc', grad_scores, key_heads) * score_scale).reshape(BLOCK, -1).astype(jnp.bfloat16)
        key_term = (jnp.einsum('hqk,qhc->khc', grad_scores, query_heads) * score_scale).reshape(key_span, -1)
        key_grads = lax.dynamic_update_slice_in_dim(key_grads, lax.dynamic_slice_in_dim(key_grads, first_row, key_span, 0) + key_term, first_row, 0)
        value_grads = lax.dynamic_update_slice_in_dim(value_grads, lax.dynamic_slice_in_dim(value_grads, first_row, key_span, 0) + value_term, first_row, 0)
        return ((key_grads, value_grads), (attn_rows, query_rows))
    zero_rows = jnp.zeros((node_count + 2 * NODE_DEV, query.shape[1]), jnp.float32)
    block_ids = jnp.arange(node_count // BLOCK, dtype=jnp.int32)
    (key_grads, value_grads), (attn_rows, query_rows) = lax.scan(one_block, (zero_rows, zero_rows), block_ids)
    attn_out = attn_rows.reshape(node_count, -1)
    grad_query = query_rows.reshape(node_count, -1)
    grad_key = key_grads[NODE_DEV:NODE_DEV + node_count].astype(jnp.bfloat16)
    grad_value = value_grads[NODE_DEV:NODE_DEV + node_count].astype(jnp.bfloat16)
    return (attn_out, grad_query, grad_key, grad_value)

def reference(node_states, query, key, value, out_weight, dec_weight, target, area_weight, var_weight, edges, edge_weight, windows):
    members = node_states.shape[0]

    def predict(states):
        latent = decode(states, edges, edge_weight)
        return lax.dot_general(dec_weight, latent, (((1,), (1,)), ((), ())), preferred_element_type=jnp.float32).astype(jnp.bfloat16)
    prediction = lax.map(predict, node_states)
    weights = area_weight[None, :] * var_weight[:, None]

    def member_grad(own_preds):
        own_values = own_preds.astype(jnp.float32)
        pair_sum = jnp.zeros_like(own_values)
        for other in range(members):
            pair_sum = pair_sum + smooth_slope(own_values - prediction[other].astype(jnp.float32))
        slopes = smooth_slope(own_values - target) - pair_sum / (members - 1)
        return (weights * slopes).astype(jnp.bfloat16)
    grad_prediction = lax.map(member_grad, prediction)

    def one_member(totals, inputs):
        wo_total, dec_total = totals
        states, member_grads, query_m, key_m, value_m = inputs
        latent = decode(states, edges, edge_weight)
        grad_latent = lax.dot_general(member_grads, dec_weight, (((0,), (0,)), ((), ())), preferred_element_type=jnp.float32)
        dec_total = dec_total + lax.dot_general(member_grads, latent, (((1,), (0,)), ((), ())), preferred_element_type=jnp.float32)
        node_sum = jnp.zeros((states.shape[0], states.shape[1]), jnp.float32)
        for edge_slot in range(edges.shape[0]):
            node_sum = node_sum.at[edges[edge_slot]].add(edge_weight[edge_slot][:, None] * grad_latent)
        grad_states = node_sum.astype(jnp.bfloat16)
        attn_out, grad_query, grad_key, grad_value = attention_grads(query_m, key_m, value_m, grad_states, out_weight, windows)
        wo_total = wo_total + lax.dot_general(attn_out, grad_states, (((0,), (0,)), ((), ())), preferred_element_type=jnp.float32)
        return ((wo_total, dec_total), (grad_states, grad_query, grad_key, grad_value))
    start_totals = (jnp.zeros((query.shape[2], node_states.shape[2]), jnp.float32), jnp.zeros((dec_weight.shape[0], dec_weight.shape[1]), jnp.float32))
    (grad_wo, grad_dec), (grad_states, grad_query, grad_key, grad_value) = lax.scan(one_member, start_totals, (node_states, grad_prediction, query, key, value))
    return (grad_states, grad_query, grad_key, grad_value, grad_wo, grad_dec)
```

```python
import functools
import math

import jax
import jax.numpy as jnp
from jax import lax
from jax.experimental import pallas as pl
from jax.experimental.pallas import tpu as pltpu
from jax.sharding import Mesh
from jax.sharding import PartitionSpec as P

HEADS = 8
HEAD_DIM = 64
PAIR = 2 * HEAD_DIM
VARS = 100
VARS_SUB = 112
VARS_LANE = 128
MEMBERS = 8
NODES = 128
POINTS = 1024
SPAN = 3 * NODES
WIDTH = 1024
ATT = 512
SMOOTH_SQUARE = 0.0625
MASKED_SCORE = -1e30
SCALE = 1.0 / math.sqrt(HEAD_DIM)

AXES = ("zh", "y", "x", "zl", "c")
SIZES = (2, 4, 4, 8, 2)
ENS = ("zh", "y")
SPACE = ("x", "zl", "c")
NEAR = ("y", "x", "c")
NEAR_SIZE = 32
FAR = ("zh", "zl")
FAR_SIZE = 16
DEC_ROWS = WIDTH // NEAR_SIZE
WO_ROWS = ATT // NEAR_SIZE
ROWS = DEC_ROWS + WO_ROWS

F32 = jnp.float32
BF16 = jnp.bfloat16
NN = (((1,), (0,)), ((), ()))
NT = (((1,), (1,)), ((), ()))
TN = (((0,), (0,)), ((), ()))


def dot(a, b, dims):
    return lax.dot_general(a, b, dims, preferred_element_type=F32)


def call(body, out_shape, scratch=(), smem=(), flops=10**8, moved=10**6, exps=0, n_in=0):
    specs = [
        pl.BlockSpec(memory_space=pltpu.SMEM if i in smem else pltpu.VMEM) for i in range(n_in)
    ]
    return pl.pallas_call(
        body,
        out_shape=out_shape,
        in_specs=specs,
        scratch_shapes=list(scratch),
        compiler_params=pltpu.CompilerParams(vmem_limit_bytes=40 * 2**20),
        cost_estimate=pl.CostEstimate(flops=flops, bytes_accessed=moved, transcendentals=exps),
    )


def shape(dims, dtype):
    return jax.ShapeDtypeStruct(dims, dtype)


def smooth_slope(t):
    return t * lax.rsqrt(t * t + SMOOTH_SQUARE)


def split(x):
    high = x.astype(BF16)
    return high, (x - high.astype(F32)).astype(BF16)


def project_body(states_ref, dec_ref, key_ref, value_ref, proj_ref, kv_ref, dec_s):
    dec_s[...] = jnp.zeros(dec_s.shape, BF16)
    dec_s[0:VARS, :] = dec_ref[...]
    proj = dot(dec_s[...], states_ref[0], NT).astype(BF16)
    for member in range(MEMBERS):
        proj_ref[member] = proj
    kv_ref[:, 0:ATT] = key_ref[0]
    kv_ref[:, ATT : 2 * ATT] = value_ref[0]


def weights_body(band_ref, edges_ref, edge_weight_ref, area_ref, var_ref, mix_ref, weight_ref):
    base = (band_ref[0] - 1) * NODES
    local = edges_ref[...] - base
    for part in range(SPAN // NODES):
        place = lax.broadcasted_iota(jnp.int32, (NODES, POINTS), 0) + part * NODES
        mix = jnp.zeros((NODES, POINTS), F32)
        for slot in range(3):
            mix = mix + jnp.where(
                local[slot : slot + 1, :] == place, edge_weight_ref[slot : slot + 1, :], 0.0
            )
        mix_ref[part * NODES : (part + 1) * NODES, :] = mix.astype(BF16)
    row = jnp.concatenate([var_ref[...], jnp.zeros((1, VARS_LANE - VARS), F32)], axis=1)
    column = jnp.transpose(jnp.broadcast_to(row, (VARS_LANE, VARS_LANE)))[0:VARS_SUB, 0:1]
    weight_ref[...] = column * area_ref[...]


def crps_body(
    member_ref,
    low_ref,
    mid_ref,
    high_ref,
    mix_ref,
    weight_ref,
    target_ref,
    own_ref,
    below_ref,
    above_ref,
    pred_s,
    grad_s,
):
    mix = mix_ref[...]
    for member in range(MEMBERS):
        proj = jnp.concatenate([low_ref[member], mid_ref[member], high_ref[member]], axis=1)
        pred_s[member] = dot(proj, mix, NN)
    grad_s[...] = jnp.zeros(grad_s.shape, BF16)
    me = member_ref[0]
    for first in range(0, VARS, 16):
        rows = min(16, VARS - first)
        mine = pred_s[me, first : first + rows, :]
        total = jnp.zeros_like(mine)
        for member in range(MEMBERS):
            total = total + smooth_slope(mine - pred_s[member, first : first + rows, :])
        slopes = smooth_slope(mine - target_ref[first : first + rows, :]) - total * (
            1.0 / (MEMBERS - 1)
        )
        grad_s[first : first + rows, :] = (weight_ref[first : first + rows, :] * slopes).astype(
            BF16
        )
    sums = dot(mix, grad_s[...], NT)
    below_ref[...] = sums[0:NODES]
    own_ref[...] = sums[NODES : 2 * NODES]
    above_ref[...] = sums[2 * NODES : SPAN]


def terms_body(own_ref, low_ref, high_ref, states_ref, attn_ref, total_ref, out_ref):
    total = own_ref[...] + low_ref[...] + high_ref[...]
    total_ref[...] = total
    parts = jnp.concatenate(split(total), axis=0)
    states = states_ref[0]
    dec = dot(jnp.concatenate([states, states], axis=0), parts, TN)
    out_ref[:, 0:DEC_ROWS, :] = dec.astype(BF16).reshape(NEAR_SIZE, DEC_ROWS, VARS_LANE)
    attn = attn_ref[...]
    wo = dot(jnp.concatenate([attn, attn], axis=0), parts, TN)
    out_ref[:, DEC_ROWS:ROWS, :] = wo.astype(BF16).reshape(NEAR_SIZE, WO_ROWS, VARS_LANE)


def sum_body(copies, in_ref, out_ref):
    total = in_ref[0].astype(F32)
    for i in range(1, in_ref.shape[0]):
        total = total + in_ref[i].astype(F32)
    total = total.astype(BF16)
    for i in range(copies):
        out_ref[i] = total


def final_body(band_ref, all_ref, dec_ref, wo_ref, grad_dec_ref, dec_s, wo_s):
    dec_s[...] = jnp.zeros(dec_s.shape, BF16)
    dec_s[0:VARS, :] = dec_ref[...]
    band = band_ref[0]
    rows = all_ref[lax.div(band, 2), DEC_ROWS:ROWS, :]
    wo_s[...] = dot(rows, dec_s[...], NN)
    wo_ref[...] = wo_s[pl.ds(pl.multiple_of(lax.rem(band, 2) * 8, 8), 8), :]
    dec = all_ref[:, 0:DEC_ROWS, :].astype(F32).reshape(WIDTH, VARS_LANE)
    grad_dec_ref[...] = jnp.transpose(dec)[0:VARS, :]


def pair_masks(dtype):
    lane = lax.broadcasted_iota(jnp.int32, (1, PAIR), 1)
    return (lane < HEAD_DIM).astype(dtype), (lane >= HEAD_DIM).astype(dtype)


def forward_body(
    band_ref, windows_ref, query_ref, low_ref, mid_ref, high_ref, prob_ref, attn_ref
):
    base = (band_ref[0] - 1) * NODES
    place = lax.broadcasted_iota(jnp.int32, (1, SPAN), 1) + base
    inside = (place >= windows_ref[0, 0]) & (place < windows_ref[1, 0])
    masks = pair_masks(BF16)
    lane = lax.broadcasted_iota(jnp.int32, (1, PAIR), 1)
    for pair in range(HEADS // 2):
        cols = slice(pair * PAIR, (pair + 1) * PAIR)
        vcols = slice(ATT + pair * PAIR, ATT + (pair + 1) * PAIR)
        query = query_ref[0, :, cols]
        keys = jnp.concatenate([r[:, cols] for r in (low_ref, mid_ref, high_ref)], axis=0)
        values = jnp.concatenate([r[:, vcols] for r in (low_ref, mid_ref, high_ref)], axis=0)
        outs = []
        for half in range(2):
            scores = dot(query * masks[half], keys, NT) * SCALE
            scores = jnp.where(inside, scores, MASKED_SCORE)
            exponent = jnp.exp(scores - jnp.max(scores, axis=-1, keepdims=True))
            prob = exponent / jnp.sum(exponent, axis=-1, keepdims=True)
            prob_ref[2 * pair + half] = prob
            outs.append(dot(prob.astype(BF16), values, NN))
        attn_ref[:, cols] = jnp.where(lane < HEAD_DIM, outs[0], outs[1]).astype(BF16)


def backward_body(
    total_ref,
    dec_ref,
    out_weight_ref,
    query_ref,
    low_ref,
    mid_ref,
    high_ref,
    prob_ref,
    states_ref,
    grad_query_ref,
    own_ref,
    below_ref,
    above_ref,
    dec_s,
):
    dec_s[...] = jnp.zeros(dec_s.shape, BF16)
    dec_s[0:VARS, :] = dec_ref[...]
    dec = dec_s[...]
    grad_states = dot(
        jnp.concatenate(split(total_ref[...]), axis=1), jnp.concatenate([dec, dec], axis=0), NN
    ).astype(BF16)
    states_ref[0] = grad_states
    grad_out = dot(grad_states, out_weight_ref[...], NT).astype(BF16)
    masks = pair_masks(BF16)
    lane = lax.broadcasted_iota(jnp.int32, (1, PAIR), 1)
    first = lane < HEAD_DIM
    for pair in range(HEADS // 2):
        cols = slice(pair * PAIR, (pair + 1) * PAIR)
        vcols = slice(ATT + pair * PAIR, ATT + (pair + 1) * PAIR)
        query = query_ref[0, :, cols]
        keys = jnp.concatenate([r[:, cols] for r in (low_ref, mid_ref, high_ref)], axis=0)
        values = jnp.concatenate([r[:, vcols] for r in (low_ref, mid_ref, high_ref)], axis=0)
        grads = grad_out[:, cols]
        key_terms, value_terms, query_terms = [], [], []
        for half in range(2):
            prob = prob_ref[2 * pair + half]
            grad_prob = dot(grads * masks[half], values, NT)
            delta = jnp.sum(prob * grad_prob, axis=-1, keepdims=True)
            grad_scores = (prob * (grad_prob - delta)).astype(BF16)
            value_terms.append(dot(prob.astype(BF16), grads, TN))
            query_terms.append(dot(grad_scores, keys, NN))
            key_terms.append(dot(grad_scores, query, TN))
        grad_query_ref[0, :, cols] = (
            jnp.where(first, query_terms[0], query_terms[1]) * SCALE
        ).astype(BF16)
        key_term = jnp.where(first, key_terms[0], key_terms[1]) * SCALE
        value_term = jnp.where(first, value_terms[0], value_terms[1])
        for term, where in ((key_term, cols), (value_term, vcols)):
            below_ref[:, where] = term[0:NODES].astype(BF16)
            own_ref[:, where] = term[NODES : 2 * NODES]
            above_ref[:, where] = term[2 * NODES : SPAN].astype(BF16)


def join_body(own_ref, low_ref, high_ref, key_ref, value_ref):
    key_ref[0] = (
        own_ref[:, 0:ATT] + low_ref[:, 0:ATT].astype(F32) + high_ref[:, 0:ATT].astype(F32)
    ).astype(BF16)
    value_ref[0] = (
        own_ref[:, ATT : 2 * ATT]
        + low_ref[:, ATT : 2 * ATT].astype(F32)
        + high_ref[:, ATT : 2 * ATT].astype(F32)
    ).astype(BF16)


def up(x):
    count = 64
    return lax.ppermute(x, SPACE, [(i, i + 1) for i in range(count - 1)])


def down(x):
    count = 64
    return lax.ppermute(x, SPACE, [(i + 1, i) for i in range(count - 1)])


def exchange(x, axes):
    return lax.all_to_all(x, axes, split_axis=0, concat_axis=0, tiled=True)


def per_device(
    node_states,
    query,
    key,
    value,
    out_weight,
    dec_weight,
    target,
    area_weight,
    var_weight,
    edges,
    edge_weight,
    windows,
):
    band = lax.axis_index(SPACE).astype(jnp.int32).reshape(1)
    member = lax.axis_index(ENS).astype(jnp.int32).reshape(1)
    proj, kv = call(
        project_body,
        (shape((MEMBERS, VARS_SUB, NODES), BF16), shape((NODES, 2 * ATT), BF16)),
        scratch=[pltpu.VMEM((VARS_SUB, WIDTH), BF16)],
        n_in=4,
    )(node_states, dec_weight, key, value)
    proj_mid = exchange(proj, ENS)
    kv_low, kv_high = up(kv), down(kv)
    proj_low, proj_high = up(proj_mid), down(proj_mid)
    mix, weight = call(
        weights_body,
        (shape((SPAN, POINTS), BF16), shape((VARS_SUB, POINTS), F32)),
        smem=(0,),
        n_in=5,
    )(band, edges, edge_weight, area_weight.reshape(1, -1), var_weight.reshape(1, -1))
    prob, attn = call(
        forward_body,
        (shape((HEADS, NODES, SPAN), F32), shape((NODES, ATT), BF16)),
        smem=(0, 1),
        n_in=6,
        exps=10**6,
    )(band, windows, query, kv_low, kv, kv_high)
    block = shape((NODES, VARS_LANE), F32)
    own, below, above = call(
        crps_body,
        (block, block, block),
        scratch=[
            pltpu.VMEM((MEMBERS, VARS_SUB, POINTS), F32),
            pltpu.VMEM((VARS_LANE, POINTS), BF16),
        ],
        smem=(0,),
        n_in=7,
    )(member, proj_low, proj_mid, proj_high, mix, weight, target)
    total, terms = call(
        terms_body,
        (block, shape((NEAR_SIZE, ROWS, VARS_LANE), BF16)),
        n_in=5,
    )(own, up(above), down(below), node_states, attn)
    near = exchange(terms, NEAR)
    copies = call(
        functools.partial(sum_body, FAR_SIZE), shape((FAR_SIZE, ROWS, VARS_LANE), BF16), n_in=1
    )(near)
    far = exchange(copies, FAR)
    copies = call(
        functools.partial(sum_body, NEAR_SIZE), shape((NEAR_SIZE, ROWS, VARS_LANE), BF16), n_in=1
    )(far)
    everything = exchange(copies, NEAR)
    grad_wo, grad_dec = call(
        final_body,
        (shape((8, WIDTH), F32), shape((VARS, WIDTH), F32)),
        scratch=[pltpu.VMEM((VARS_LANE, WIDTH), BF16), pltpu.VMEM((WO_ROWS, WIDTH), F32)],
        smem=(0,),
        n_in=3,
    )(band, everything, dec_weight)
    wide = (NODES, 2 * ATT)
    grad_states, grad_query, kv_own, kv_below, kv_above = call(
        backward_body,
        (
            shape((1, NODES, WIDTH), BF16),
            shape((1, NODES, ATT), BF16),
            shape(wide, F32),
            shape(wide, BF16),
            shape(wide, BF16),
        ),
        scratch=[pltpu.VMEM((VARS_LANE, WIDTH), BF16)],
        n_in=8,
        flops=10**9,
        moved=10**7,
    )(total, dec_weight, out_weight, query, kv_low, kv, kv_high, prob)
    grad_key, grad_value = call(
        join_body, (shape((1, NODES, ATT), BF16), shape((1, NODES, ATT), BF16)), n_in=3
    )(kv_own, up(kv_above), down(kv_below))
    return grad_states, grad_query, grad_key, grad_value, grad_wo, grad_dec


def solution(mesh):
    fine = Mesh(mesh.devices.reshape(SIZES), AXES)
    in_specs = (
        P(ENS, SPACE, None),
        P(ENS, SPACE, None),
        P(ENS, SPACE, None),
        P(ENS, SPACE, None),
        P(),
        P(),
        P(None, SPACE),
        P(SPACE),
        P(),
        P(None, SPACE),
        P(None, SPACE),
        P(None, SPACE),
    )
    out_specs = (
        P(ENS, SPACE, None),
        P(ENS, SPACE, None),
        P(ENS, SPACE, None),
        P(ENS, SPACE, None),
        P(SPACE, None),
        P(),
    )
    return jax.shard_map(
        per_device, mesh=fine, in_specs=in_specs, out_specs=out_specs, check_vma=False
    )
```

```python
import functools
import math

import jax
import jax.numpy as jnp
from jax import lax
from jax.experimental import pallas as pl
from jax.experimental.pallas import tpu as pltpu
from jax.sharding import Mesh
from jax.sharding import PartitionSpec as P

HEADS = 8
HEAD_DIM = 64
PAIR = 2 * HEAD_DIM
VARS = 100
VARS_SUB = 112
VARS_LANE = 128
MEMBERS = 8
NODES = 128
POINTS = 1024
SPAN = 3 * NODES
WIDTH = 1024
ATT = 512
SMOOTH_SQUARE = 0.0625
MASKED_SCORE = -1e30
SCALE = 1.0 / math.sqrt(HEAD_DIM)

AXES = ("zh", "y", "x", "zl", "c")
SIZES = (2, 4, 4, 8, 2)
ENS = ("zh", "y")
SPACE = ("x", "zl", "c")
NEAR = ("y", "x", "c")
NEAR_SIZE = 32
FAR = ("zh", "zl")
FAR_SIZE = 16
DEC_ROWS = WIDTH // NEAR_SIZE
WO_ROWS = ATT // NEAR_SIZE
ROWS = DEC_ROWS + WO_ROWS

F32 = jnp.float32
BF16 = jnp.bfloat16
NN = (((1,), (0,)), ((), ()))
NT = (((1,), (1,)), ((), ()))
TN = (((0,), (0,)), ((), ()))


def dot(a, b, dims):
    return lax.dot_general(a, b, dims, preferred_element_type=F32)


def call(body, out_shape, spaces, scratch=(), limit=24 * 2**20, exps=0):
    kinds = {
        "s": pl.BlockSpec(memory_space=pltpu.SMEM),
        "v": pl.BlockSpec(memory_space=pltpu.VMEM),
        "a": pl.BlockSpec(memory_space=pl.ANY),
        "h": pl.BlockSpec(memory_space=pltpu.HBM),
    }
    specs = [kinds[space] for space in spaces]
    return pl.pallas_call(
        body,
        out_shape=out_shape,
        in_specs=specs,
        scratch_shapes=list(scratch),
        compiler_params=pltpu.CompilerParams(vmem_limit_bytes=limit),
        cost_estimate=pl.CostEstimate(flops=10**8, bytes_accessed=10**6, transcendentals=exps),
    )


def shape(dims, dtype):
    return jax.ShapeDtypeStruct(dims, dtype)


def smooth_slope(t):
    return t * lax.rsqrt(t * t + SMOOTH_SQUARE)


def split(x):
    high = x.astype(BF16)
    return high, (x - high.astype(F32)).astype(BF16)


def project_body(
    states_hbm, dec_hbm, key_hbm, value_hbm, proj_ref, kv_ref, states_s, dec_s, pad_s, sems
):
    copies = [
        pltpu.make_async_copy(states_hbm.at[0], states_s, sems.at[0]),
        pltpu.make_async_copy(dec_hbm, dec_s, sems.at[1]),
    ]
    for block in range(ATT // PAIR):
        cols = pl.ds(block * PAIR, PAIR)
        for source, first in ((key_hbm, 0), (value_hbm, ATT // PAIR)):
            copies.append(
                pltpu.make_async_copy(
                    source.at[0, :, cols], kv_ref.at[first + block], sems.at[len(copies)]
                )
            )
    for copy in copies:
        copy.start()
    pad_s[...] = jnp.zeros(pad_s.shape, BF16)
    copies[1].wait()
    pad_s[0:VARS, :] = dec_s[...]
    copies[0].wait()
    proj = dot(pad_s[...], states_s[...], NT).astype(BF16)
    for member in range(MEMBERS):
        proj_ref[member] = proj
    for copy in copies[2:]:
        copy.wait()


def weights_body(band_ref, edges_ref, edge_weight_ref, area_ref, var_ref, mix_ref, weight_ref):
    base = (band_ref[0] - 1) * NODES
    local = edges_ref[...] - base
    for part in range(SPAN // NODES):
        place = lax.broadcasted_iota(jnp.int32, (NODES, POINTS), 0) + part * NODES
        mix = jnp.zeros((NODES, POINTS), F32)
        for slot in range(3):
            mix = mix + jnp.where(
                local[slot : slot + 1, :] == place, edge_weight_ref[slot : slot + 1, :], 0.0
            )
        mix_ref[part * NODES : (part + 1) * NODES, :] = mix.astype(BF16)
    row = jnp.concatenate([var_ref[...], jnp.zeros((1, VARS_LANE - VARS), F32)], axis=1)
    column = jnp.transpose(jnp.broadcast_to(row, (VARS_LANE, VARS_LANE)))[0:VARS_SUB, 0:1]
    weight_ref[...] = column * area_ref[...]


def crps_body(
    member_ref,
    low_ref,
    mid_ref,
    high_ref,
    mix_ref,
    weight_ref,
    target_ref,
    own_ref,
    below_ref,
    above_ref,
    pred_s,
    grad_s,
):
    mix = mix_ref[...]
    for member in range(MEMBERS):
        rows = slice(member * VARS_SUB, (member + 1) * VARS_SUB)
        proj = jnp.concatenate([low_ref[rows], mid_ref[member], high_ref[rows]], axis=1)
        pred_s[member] = dot(proj, mix, NN)
    grad_s[...] = jnp.zeros(grad_s.shape, BF16)
    me = member_ref[0]
    for first in range(0, VARS, 16):
        rows = min(16, VARS - first)
        mine = pred_s[me, first : first + rows, :]
        total = jnp.zeros_like(mine)
        for member in range(MEMBERS):
            total = total + smooth_slope(mine - pred_s[member, first : first + rows, :])
        slopes = smooth_slope(mine - target_ref[first : first + rows, :]) - total * (
            1.0 / (MEMBERS - 1)
        )
        grad_s[first : first + rows, :] = (weight_ref[first : first + rows, :] * slopes).astype(
            BF16
        )
    sums = dot(mix, grad_s[...], NT)
    below_ref[...] = sums[0:NODES]
    own_ref[...] = sums[NODES : 2 * NODES]
    above_ref[...] = sums[2 * NODES : SPAN]


def terms_body(own_ref, low_ref, high_ref, states_ref, attn_ref, total_ref, out_ref):
    total = own_ref[...] + low_ref[...] + high_ref[...]
    total_ref[...] = total
    parts = jnp.concatenate(split(total), axis=0)
    states = states_ref[0]
    dec = dot(jnp.concatenate([states, states], axis=0), parts, TN)
    out_ref[:, 0:DEC_ROWS, :] = dec.astype(BF16).reshape(NEAR_SIZE, DEC_ROWS, VARS_LANE)
    attn = attn_ref[...]
    wo = dot(jnp.concatenate([attn, attn], axis=0), parts, TN)
    out_ref[:, DEC_ROWS:ROWS, :] = wo.astype(BF16).reshape(NEAR_SIZE, WO_ROWS, VARS_LANE)


def sum_body(copies, in_ref, *rest):
    out_ref = rest[-1]
    total = in_ref[0].astype(F32)
    for i in range(1, in_ref.shape[0]):
        total = total + in_ref[i].astype(F32)
    total = total.astype(BF16)
    for i in range(copies):
        out_ref[i] = total


def final_body(band_ref, all_ref, dec_ref, wo_ref, grad_dec_ref, dec_s, wo_s):
    dec_s[...] = jnp.zeros(dec_s.shape, BF16)
    dec_s[0:VARS, :] = dec_ref[...]
    band = band_ref[0]
    rows = all_ref[lax.div(band, 2), DEC_ROWS:ROWS, :]
    wo_s[...] = dot(rows, dec_s[...], NN)
    wo_ref[...] = wo_s[pl.ds(pl.multiple_of(lax.rem(band, 2) * 8, 8), 8), :]
    dec = all_ref[:, 0:DEC_ROWS, :].astype(F32).reshape(WIDTH, VARS_LANE)
    grad_dec_ref[...] = jnp.transpose(dec)[0:VARS, :]


def pair_masks(dtype):
    lane = lax.broadcasted_iota(jnp.int32, (1, PAIR), 1)
    return (lane < HEAD_DIM).astype(dtype), (lane >= HEAD_DIM).astype(dtype)


def band_blocks(low_ref, mid_ref, high_ref, block):
    first = MEMBERS * VARS_SUB + block * NODES
    rows = slice(first, first + NODES)
    return jnp.concatenate([low_ref[rows], mid_ref[block], high_ref[rows]], axis=0)


def forward_body(
    band_ref, windows_ref, query_ref, low_ref, mid_ref, high_ref, prob_ref, attn_ref
):
    base = (band_ref[0] - 1) * NODES
    place = lax.broadcasted_iota(jnp.int32, (1, SPAN), 1) + base
    inside = (place >= windows_ref[0, 0]) & (place < windows_ref[1, 0])
    masks = pair_masks(BF16)
    lane = lax.broadcasted_iota(jnp.int32, (1, PAIR), 1)
    for pair in range(HEADS // 2):
        cols = slice(pair * PAIR, (pair + 1) * PAIR)
        query = query_ref[0, :, cols]
        keys = band_blocks(low_ref, mid_ref, high_ref, pair)
        values = band_blocks(low_ref, mid_ref, high_ref, HEADS // 2 + pair)
        outs = []
        for half in range(2):
            scores = dot(query * masks[half], keys, NT) * SCALE
            scores = jnp.where(inside, scores, MASKED_SCORE)
            exponent = jnp.exp(scores - jnp.max(scores, axis=-1, keepdims=True))
            prob = exponent / jnp.sum(exponent, axis=-1, keepdims=True)
            prob_ref[2 * pair + half] = prob
            outs.append(dot(prob.astype(BF16), values, NN))
        attn_ref[:, cols] = jnp.where(lane < HEAD_DIM, outs[0], outs[1]).astype(BF16)


def backward_body(
    total_ref,
    dec_ref,
    out_weight_ref,
    query_ref,
    low_ref,
    mid_ref,
    high_ref,
    prob_ref,
    after_ref,
    states_ref,
    grad_query_ref,
    own_ref,
    below_ref,
    above_ref,
    dec_s,
):
    dec_s[...] = jnp.zeros(dec_s.shape, BF16)
    dec_s[0:VARS, :] = dec_ref[...]
    dec = dec_s[...]
    grad_states = dot(
        jnp.concatenate(split(total_ref[...]), axis=1), jnp.concatenate([dec, dec], axis=0), NN
    ).astype(BF16)
    states_ref[0] = grad_states
    grad_out = dot(grad_states, out_weight_ref[...], NT).astype(BF16)
    masks = pair_masks(BF16)
    lane = lax.broadcasted_iota(jnp.int32, (1, PAIR), 1)
    first = lane < HEAD_DIM
    for pair in range(HEADS // 2):
        cols = slice(pair * PAIR, (pair + 1) * PAIR)
        vcols = slice(ATT + pair * PAIR, ATT + (pair + 1) * PAIR)
        query = query_ref[0, :, cols]
        keys = band_blocks(low_ref, mid_ref, high_ref, pair)
        values = band_blocks(low_ref, mid_ref, high_ref, HEADS // 2 + pair)
        grads = grad_out[:, cols]
        key_terms, value_terms, query_terms = [], [], []
        for half in range(2):
            prob = prob_ref[2 * pair + half]
            grad_prob = dot(grads * masks[half], values, NT)
            delta = jnp.sum(prob * grad_prob, axis=-1, keepdims=True)
            grad_scores = (prob * (grad_prob - delta)).astype(BF16)
            value_terms.append(dot(prob.astype(BF16), grads, TN))
            query_terms.append(dot(grad_scores, keys, NN))
            key_terms.append(dot(grad_scores, query, TN))
        grad_query_ref[0, :, cols] = (
            jnp.where(first, query_terms[0], query_terms[1]) * SCALE
        ).astype(BF16)
        key_term = jnp.where(first, key_terms[0], key_terms[1]) * SCALE
        value_term = jnp.where(first, value_terms[0], value_terms[1])
        for term, where in ((key_term, cols), (value_term, vcols)):
            below_ref[:, where] = term[0:NODES].astype(BF16)
            own_ref[:, where] = term[NODES : 2 * NODES]
            above_ref[:, where] = term[2 * NODES : SPAN].astype(BF16)


def join_body(own_ref, low_ref, high_ref, key_ref, value_ref, done_ref):
    done_ref[...] = jnp.zeros(done_ref.shape, F32)
    key_ref[0] = (
        own_ref[:, 0:ATT] + low_ref[:, 0:ATT].astype(F32) + high_ref[:, 0:ATT].astype(F32)
    ).astype(BF16)
    value_ref[0] = (
        own_ref[:, ATT : 2 * ATT]
        + low_ref[:, ATT : 2 * ATT].astype(F32)
        + high_ref[:, ATT : 2 * ATT].astype(F32)
    ).astype(BF16)


def up(x):
    count = 64
    return lax.ppermute(x, SPACE, [(i, i + 1) for i in range(count - 1)])


def down(x):
    count = 64
    return lax.ppermute(x, SPACE, [(i + 1, i) for i in range(count - 1)])


def exchange(x, axes):
    return lax.all_to_all(x, axes, split_axis=0, concat_axis=0, tiled=True)


def per_device(
    node_states,
    query,
    key,
    value,
    out_weight,
    dec_weight,
    target,
    area_weight,
    var_weight,
    edges,
    edge_weight,
    windows,
):
    band = lax.axis_index(SPACE).astype(jnp.int32).reshape(1)
    member = lax.axis_index(ENS).astype(jnp.int32).reshape(1)
    blocks = 2 * ATT // PAIR
    proj, kv = call(
        project_body,
        (shape((MEMBERS, VARS_SUB, NODES), BF16), shape((blocks, NODES, PAIR), BF16)),
        "hhhh",
        scratch=[
            pltpu.VMEM((NODES, WIDTH), BF16),
            pltpu.VMEM((VARS, WIDTH), BF16),
            pltpu.VMEM((VARS_SUB, WIDTH), BF16),
            pltpu.SemaphoreType.DMA((2 + blocks,)),
        ],
        limit=None,
    )(node_states, dec_weight, key, value)
    mid = exchange(proj, ENS)
    packed = jnp.concatenate([mid.reshape(-1, NODES), kv.reshape(-1, PAIR)], axis=0)
    low, high = up(packed), down(packed)
    mix, weight = call(
        weights_body,
        (shape((SPAN, POINTS), BF16), shape((VARS_SUB, POINTS), F32)),
        "svvvv",
    )(band, edges, edge_weight, area_weight.reshape(1, -1), var_weight.reshape(1, -1))
    prob, attn = call(
        forward_body,
        (shape((HEADS, NODES, SPAN), F32), shape((NODES, ATT), BF16)),
        "ssvvvv",
        exps=10**6,
    )(band, windows, query, low, kv, high)
    block = shape((NODES, VARS_LANE), F32)
    own, below, above = call(
        crps_body,
        (block, block, block),
        "svvvvvv",
        scratch=[
            pltpu.VMEM((MEMBERS, VARS_SUB, POINTS), F32),
            pltpu.VMEM((VARS_LANE, POINTS), BF16),
        ],
    )(member, low, mid, high, mix, weight, target)
    total, terms = call(
        terms_body,
        (block, shape((NEAR_SIZE, ROWS, VARS_LANE), BF16)),
        "vvvvv",
    )(own, up(above), down(below), node_states, attn)
    near = exchange(terms, NEAR)
    near_sums = call(
        functools.partial(sum_body, FAR_SIZE), shape((FAR_SIZE, ROWS, VARS_LANE), BF16), "v"
    )(near)
    far = exchange(near_sums, FAR)
    wide = (NODES, 2 * ATT)
    grad_states, grad_query, kv_own, kv_below, kv_above = call(
        backward_body,
        (
            shape((1, NODES, WIDTH), BF16),
            shape((1, NODES, ATT), BF16),
            shape(wide, F32),
            shape(wide, BF16),
            shape(wide, BF16),
        ),
        "vvvvvvvva",
        scratch=[pltpu.VMEM((VARS_LANE, WIDTH), BF16)],
    )(total, dec_weight, out_weight, query, low, kv, high, prob, near_sums)
    grad_key, grad_value, joined = call(
        join_body,
        (shape((1, NODES, ATT), BF16), shape((1, NODES, ATT), BF16), shape((8, 128), F32)),
        "vvv",
    )(kv_own, up(kv_above), down(kv_below))
    far_sums = call(
        functools.partial(sum_body, NEAR_SIZE),
        shape((NEAR_SIZE, ROWS, VARS_LANE), BF16),
        "vv",
    )(far, joined)
    everything = exchange(far_sums, NEAR)
    grad_wo, grad_dec = call(
        final_body,
        (shape((8, WIDTH), F32), shape((VARS, WIDTH), F32)),
        "svv",
        scratch=[pltpu.VMEM((VARS_LANE, WIDTH), BF16), pltpu.VMEM((WO_ROWS, WIDTH), F32)],
    )(band, everything, dec_weight)
    return grad_states, grad_query, grad_key, grad_value, grad_wo, grad_dec


def solution(mesh):
    fine = Mesh(mesh.devices.reshape(SIZES), AXES)
    in_specs = (
        P(ENS, SPACE, None),
        P(ENS, SPACE, None),
        P(ENS, SPACE, None),
        P(ENS, SPACE, None),
        P(),
        P(),
        P(None, SPACE),
        P(SPACE),
        P(),
        P(None, SPACE),
        P(None, SPACE),
        P(None, SPACE),
    )
    out_specs = (
        P(ENS, SPACE, None),
        P(ENS, SPACE, None),
        P(ENS, SPACE, None),
        P(ENS, SPACE, None),
        P(SPACE, None),
        P(),
    )
    return jax.shard_map(
        per_device, mesh=fine, in_specs=in_specs, out_specs=out_specs, check_vma=False
    )
```

```python
import functools
import math

import jax
import jax.numpy as jnp
from jax import lax
from jax.experimental import pallas as pl
from jax.experimental.pallas import tpu as pltpu
from jax.sharding import Mesh
from jax.sharding import PartitionSpec as P

HEADS = 8
HEAD_DIM = 64
PAIR = 2 * HEAD_DIM
VARS = 100
VARS_SUB = 112
VARS_LANE = 128
MEMBERS = 8
NODES = 128
POINTS = 1024
SPAN = 3 * NODES
WIDTH = 1024
ATT = 512
SMOOTH_SQUARE = 0.0625
MASKED_SCORE = -1e30
SCALE = 1.0 / math.sqrt(HEAD_DIM)

AXES = ("zh", "y", "x", "zl", "c")
SIZES = (2, 4, 4, 8, 2)
ENS = ("zh", "y")
SPACE = ("x", "zl", "c")
NEAR = ("y", "x", "c")
NEAR_SIZE = 32
FAR = ("zh", "zl")
FAR_SIZE = 16
DEC_ROWS = WIDTH // NEAR_SIZE
WO_ROWS = ATT // NEAR_SIZE
ROWS = DEC_ROWS + WO_ROWS

F32 = jnp.float32
BF16 = jnp.bfloat16
NN = (((1,), (0,)), ((), ()))
NT = (((1,), (1,)), ((), ()))
TN = (((0,), (0,)), ((), ()))


def dot(a, b, dims):
    return lax.dot_general(a, b, dims, preferred_element_type=F32)


class Landing:
    def __init__(self, source, target, sem):
        self.target = target
        self.copy = pltpu.make_async_copy(source, target, sem)
        self.copy.start()

    def ready(self):
        self.copy.wait()
        return self.target


def call(body, out_shape, spaces, args, scratch=(), limit=24 * 2**20, exps=0):
    kinds = {
        "s": pl.BlockSpec(memory_space=pltpu.SMEM),
        "v": pl.BlockSpec(memory_space=pltpu.VMEM),
        "a": pl.BlockSpec(memory_space=pl.ANY),
        "l": pl.BlockSpec(memory_space=pl.ANY),
    }
    specs = [kinds[space] for space in spaces]
    landed = [i for i, space in enumerate(spaces) if space == "l"]
    outs = len(out_shape) if isinstance(out_shape, tuple) else 1
    if landed:
        targets = [pltpu.VMEM(args[i].shape, args[i].dtype) for i in landed]
        scratch = [*targets, pltpu.SemaphoreType.DMA((len(landed),)), *scratch]

    def kernel(*refs):
        inputs, results, rest = (
            list(refs[: len(args)]),
            refs[len(args) : len(args) + outs],
            refs[len(args) + outs :],
        )
        if landed:
            count = len(landed)
            for k, i in enumerate(landed):
                inputs[i] = Landing(inputs[i], rest[k], rest[count].at[k])
            rest = rest[count + 1 :]
        body(*inputs, *results, *rest)

    return pl.pallas_call(
        kernel,
        out_shape=out_shape,
        in_specs=specs,
        scratch_shapes=list(scratch),
        compiler_params=pltpu.CompilerParams(vmem_limit_bytes=limit),
        cost_estimate=pl.CostEstimate(flops=10**8, bytes_accessed=10**6, transcendentals=exps),
    )(*args)


def shape(dims, dtype):
    return jax.ShapeDtypeStruct(dims, dtype)


def smooth_slope(t):
    return t * lax.rsqrt(t * t + SMOOTH_SQUARE)


def split(x):
    high = x.astype(BF16)
    return high, (x - high.astype(F32)).astype(BF16)


def project_body(
    states_hbm, dec_hbm, key_hbm, value_hbm, proj_ref, kv_ref, states_s, dec_s, pad_s, sems
):
    copies = [
        pltpu.make_async_copy(states_hbm.at[0], states_s, sems.at[0]),
        pltpu.make_async_copy(dec_hbm, dec_s, sems.at[1]),
    ]
    for block in range(ATT // PAIR):
        cols = pl.ds(block * PAIR, PAIR)
        for source, first in ((key_hbm, 0), (value_hbm, ATT // PAIR)):
            copies.append(
                pltpu.make_async_copy(
                    source.at[0, :, cols], kv_ref.at[first + block], sems.at[len(copies)]
                )
            )
    for copy in copies:
        copy.start()
    pad_s[...] = jnp.zeros(pad_s.shape, BF16)
    copies[1].wait()
    pad_s[0:VARS, :] = dec_s[...]
    copies[0].wait()
    proj = dot(pad_s[...], states_s[...], NT).astype(BF16)
    for member in range(MEMBERS):
        proj_ref[member] = proj
    for copy in copies[2:]:
        copy.wait()


def bases(band):
    side = 2 * lax.rem(band, 2) - 1
    return (band + side) * NODES, band * NODES, (band - side) * NODES


def weights_body(band_ref, edges_ref, edge_weight_ref, area_ref, var_ref, mix_ref, weight_ref):
    edges = edges_ref[...]
    for part, base in enumerate(bases(band_ref[0])):
        place = lax.broadcasted_iota(jnp.int32, (NODES, POINTS), 0) + base
        mix = jnp.zeros((NODES, POINTS), F32)
        for slot in range(3):
            mix = mix + jnp.where(
                edges[slot : slot + 1, :] == place, edge_weight_ref[slot : slot + 1, :], 0.0
            )
        mix_ref[part * NODES : (part + 1) * NODES, :] = mix.astype(BF16)
    row = jnp.concatenate([var_ref[...], jnp.zeros((1, VARS_LANE - VARS), F32)], axis=1)
    column = jnp.transpose(jnp.broadcast_to(row, (VARS_LANE, VARS_LANE)))[0:VARS_SUB, 0:1]
    weight_ref[...] = column * area_ref[...]


def crps_body(
    member_ref,
    far_ref,
    mid_ref,
    mate_ref,
    mix_ref,
    weight_ref,
    target_ref,
    to_far_ref,
    own_ref,
    to_mate_ref,
    pred_s,
    grad_s,
):
    mix = mix_ref[...]
    for member in range(MEMBERS):
        rows = slice(member * VARS_SUB, (member + 1) * VARS_SUB)
        proj = jnp.concatenate([far_ref[rows], mid_ref[member], mate_ref[rows]], axis=1)
        pred_s[member] = dot(proj, mix, NN)
    grad_s[...] = jnp.zeros(grad_s.shape, BF16)
    me = member_ref[0]
    for first in range(0, VARS, 16):
        rows = min(16, VARS - first)
        mine = pred_s[me, first : first + rows, :]
        total = jnp.zeros_like(mine)
        for member in range(MEMBERS):
            total = total + smooth_slope(mine - pred_s[member, first : first + rows, :])
        slopes = smooth_slope(mine - target_ref[first : first + rows, :]) - total * (
            1.0 / (MEMBERS - 1)
        )
        grad_s[first : first + rows, :] = (weight_ref[first : first + rows, :] * slopes).astype(
            BF16
        )
    sums = dot(mix, grad_s[...], NT)
    to_far_ref[...] = sums[0:NODES]
    own_ref[...] = sums[NODES : 2 * NODES]
    to_mate_ref[...] = sums[2 * NODES : SPAN]


def terms_body(own_ref, far_ref, mate_ref, states_ref, attn_ref, total_ref, out_ref):
    total = own_ref.ready()[...] + far_ref.ready()[...] + mate_ref.ready()[...]
    total_ref[...] = total
    parts = jnp.concatenate(split(total), axis=0)
    states = states_ref.ready()[0]
    dec = dot(jnp.concatenate([states, states], axis=0), parts, TN)
    out_ref[:, 0:DEC_ROWS, :] = dec.astype(BF16).reshape(NEAR_SIZE, DEC_ROWS, VARS_LANE)
    attn = attn_ref.ready()[...]
    wo = dot(jnp.concatenate([attn, attn], axis=0), parts, TN)
    out_ref[:, DEC_ROWS:ROWS, :] = wo.astype(BF16).reshape(NEAR_SIZE, WO_ROWS, VARS_LANE)


def sum_body(copies, in_ref, *rest):
    out_ref = rest[-1]
    total = in_ref[0].astype(F32)
    for i in range(1, in_ref.shape[0]):
        total = total + in_ref[i].astype(F32)
    total = total.astype(BF16)
    for i in range(copies):
        out_ref[i] = total


def final_body(band_ref, all_ref, dec_ref, wo_ref, grad_dec_ref, dec_s, wo_s):
    dec_s[...] = jnp.zeros(dec_s.shape, BF16)
    dec_s[0:VARS, :] = dec_ref[...]
    band = band_ref[0]
    rows = all_ref[lax.div(band, 2), DEC_ROWS:ROWS, :]
    wo_s[...] = dot(rows, dec_s[...], NN)
    wo_ref[...] = wo_s[pl.ds(pl.multiple_of(lax.rem(band, 2) * 8, 8), 8), :]
    dec = all_ref[:, 0:DEC_ROWS, :].astype(F32).reshape(WIDTH, VARS_LANE)
    grad_dec_ref[...] = jnp.transpose(dec)[0:VARS, :]


def pair_masks(dtype):
    lane = lax.broadcasted_iota(jnp.int32, (1, PAIR), 1)
    return (lane < HEAD_DIM).astype(dtype), (lane >= HEAD_DIM).astype(dtype)


def band_blocks(far_ref, mid_ref, mate_ref, block):
    first = MEMBERS * VARS_SUB + block * NODES
    rows = slice(first, first + NODES)
    return jnp.concatenate([far_ref[rows], mid_ref[block], mate_ref[rows]], axis=0)


def forward_body(
    band_ref, windows_ref, query_ref, far_ref, mid_ref, mate_ref, prob_ref, attn_ref
):
    lanes = lax.broadcasted_iota(jnp.int32, (1, NODES), 1)
    place = jnp.concatenate([lanes + base for base in bases(band_ref[0])], axis=1)
    inside = (place >= windows_ref[0, 0]) & (place < windows_ref[1, 0])
    masks = pair_masks(BF16)
    lane = lax.broadcasted_iota(jnp.int32, (1, PAIR), 1)
    for pair in range(HEADS // 2):
        cols = slice(pair * PAIR, (pair + 1) * PAIR)
        query = query_ref[0, :, cols]
        keys = band_blocks(far_ref, mid_ref, mate_ref, pair)
        values = band_blocks(far_ref, mid_ref, mate_ref, HEADS // 2 + pair)
        outs = []
        for half in range(2):
            scores = dot(query * masks[half], keys, NT) * SCALE
            scores = jnp.where(inside, scores, MASKED_SCORE)
            exponent = jnp.exp(scores - jnp.max(scores, axis=-1, keepdims=True))
            prob = exponent / jnp.sum(exponent, axis=-1, keepdims=True)
            prob_ref[2 * pair + half] = prob
            outs.append(dot(prob.astype(BF16), values, NN))
        attn_ref[:, cols] = jnp.where(lane < HEAD_DIM, outs[0], outs[1]).astype(BF16)


def backward_body(
    total_ref,
    dec_ref,
    out_weight_ref,
    query_ref,
    far_ref,
    mid_ref,
    mate_ref,
    prob_ref,
    states_ref,
    grad_query_ref,
    to_far_ref,
    own_ref,
    to_mate_ref,
    done_ref,
    dec_s,
):
    done_ref[...] = jnp.zeros(done_ref.shape, F32)
    dec_s[...] = jnp.zeros(dec_s.shape, BF16)
    dec_s[0:VARS, :] = dec_ref.ready()[...]
    dec = dec_s[...]
    grad_states = dot(
        jnp.concatenate(split(total_ref.ready()[...]), axis=1), jnp.concatenate([dec, dec], axis=0), NN
    ).astype(BF16)
    states_ref[0] = grad_states
    grad_out = dot(grad_states, out_weight_ref.ready()[...], NT).astype(BF16)
    query_ref, prob_ref = query_ref.ready(), prob_ref.ready()
    far_ref, mid_ref, mate_ref = far_ref.ready(), mid_ref.ready(), mate_ref.ready()
    masks = pair_masks(BF16)
    lane = lax.broadcasted_iota(jnp.int32, (1, PAIR), 1)
    first = lane < HEAD_DIM
    for pair in range(HEADS // 2):
        cols = slice(pair * PAIR, (pair + 1) * PAIR)
        vcols = slice(ATT + pair * PAIR, ATT + (pair + 1) * PAIR)
        query = query_ref[0, :, cols]
        keys = band_blocks(far_ref, mid_ref, mate_ref, pair)
        values = band_blocks(far_ref, mid_ref, mate_ref, HEADS // 2 + pair)
        grads = grad_out[:, cols]
        key_terms, value_terms, query_terms = [], [], []
        for half in range(2):
            prob = prob_ref[2 * pair + half]
            grad_prob = dot(grads * masks[half], values, NT)
            delta = jnp.sum(prob * grad_prob, axis=-1, keepdims=True)
            grad_scores = (prob * (grad_prob - delta)).astype(BF16)
            value_terms.append(dot(prob.astype(BF16), grads, TN))
            query_terms.append(dot(grad_scores, keys, NN))
            key_terms.append(dot(grad_scores, query, TN))
        grad_query_ref[0, :, cols] = (
            jnp.where(first, query_terms[0], query_terms[1]) * SCALE
        ).astype(BF16)
        key_term = jnp.where(first, key_terms[0], key_terms[1]) * SCALE
        value_term = jnp.where(first, value_terms[0], value_terms[1])
        for term, where in ((key_term, cols), (value_term, vcols)):
            to_far_ref[:, where] = term[0:NODES].astype(BF16)
            own_ref[:, where] = term[NODES : 2 * NODES]
            to_mate_ref[:, where] = term[2 * NODES : SPAN].astype(BF16)


def join_body(own_ref, far_ref, mate_ref, key_ref, value_ref, done_ref):
    done_ref[...] = jnp.zeros(done_ref.shape, F32)
    key_ref[0] = (
        own_ref[:, 0:ATT] + far_ref[:, 0:ATT].astype(F32) + mate_ref[:, 0:ATT].astype(F32)
    ).astype(BF16)
    value_ref[0] = (
        own_ref[:, ATT : 2 * ATT]
        + far_ref[:, ATT : 2 * ATT].astype(F32)
        + mate_ref[:, ATT : 2 * ATT].astype(F32)
    ).astype(BF16)


def swap_far(x):
    pairs = [(i, i + 1) for i in range(1, 63, 2)]
    return lax.ppermute(x, SPACE, pairs + [(target, source) for source, target in pairs])


def swap_mate(x):
    return lax.ppermute(x, "c", [(0, 1), (1, 0)])


def exchange(x, axes):
    return lax.all_to_all(x, axes, split_axis=0, concat_axis=0, tiled=True)


def per_device(
    node_states,
    query,
    key,
    value,
    out_weight,
    dec_weight,
    target,
    area_weight,
    var_weight,
    edges,
    edge_weight,
    windows,
):
    band = lax.axis_index(SPACE).astype(jnp.int32).reshape(1)
    member = lax.axis_index(ENS).astype(jnp.int32).reshape(1)
    blocks = 2 * ATT // PAIR
    proj, kv = call(
        project_body,
        (shape((MEMBERS, VARS_SUB, NODES), BF16), shape((blocks, NODES, PAIR), BF16)),
        "aaaa", (node_states, dec_weight, key, value,),
        scratch=[
            pltpu.VMEM((NODES, WIDTH), BF16),
            pltpu.VMEM((VARS, WIDTH), BF16),
            pltpu.VMEM((VARS_SUB, WIDTH), BF16),
            pltpu.SemaphoreType.DMA((2 + blocks,)),
        ],
        limit=None,
    )
    mid = exchange(proj, ENS)
    packed = jnp.concatenate([mid.reshape(-1, NODES), kv.reshape(-1, PAIR)], axis=0)
    far, mate = swap_far(packed), swap_mate(packed)
    mix, weight = call(
        weights_body,
        (shape((SPAN, POINTS), BF16), shape((VARS_SUB, POINTS), F32)),
        "svvvv", (band, edges, edge_weight, area_weight.reshape(1, -1), var_weight.reshape(1, -1),),
    )
    prob, attn = call(
        forward_body,
        (shape((HEADS, NODES, SPAN), F32), shape((NODES, ATT), BF16)),
        "ssvvvv", (band, windows, query, far, kv, mate,),
        exps=10**6,
    )
    block = shape((NODES, VARS_LANE), F32)
    to_far, own, to_mate = call(
        crps_body,
        (block, block, block),
        "svvvvvv", (member, far, mid, mate, mix, weight, target,),
        scratch=[
            pltpu.VMEM((MEMBERS, VARS_SUB, POINTS), F32),
            pltpu.VMEM((VARS_LANE, POINTS), BF16),
        ],
    )
    total, terms = call(
        terms_body,
        (block, shape((NEAR_SIZE, ROWS, VARS_LANE), BF16)),
        "lllll", (own, swap_far(to_far), swap_mate(to_mate), node_states, attn,),
    )
    near = exchange(terms, NEAR)
    wide = (NODES, 2 * ATT)
    grad_states, grad_query, kv_far, kv_own, kv_mate, done = call(
        backward_body,
        (
            shape((1, NODES, WIDTH), BF16),
            shape((1, NODES, ATT), BF16),
            shape(wide, BF16),
            shape(wide, F32),
            shape(wide, BF16),
            shape((8, 128), F32),
        ),
        "llllllll", (total, dec_weight, out_weight, query, far, kv, mate, prob,),
        scratch=[pltpu.VMEM((VARS_LANE, WIDTH), BF16)],
    )
    near_sums = call(
        functools.partial(sum_body, FAR_SIZE), shape((FAR_SIZE, ROWS, VARS_LANE), BF16), "vv", (near, done,)
    )
    along = exchange(near_sums, FAR)
    grad_key, grad_value, joined = call(
        join_body,
        (shape((1, NODES, ATT), BF16), shape((1, NODES, ATT), BF16), shape((8, 128), F32)),
        "vvv", (kv_own, swap_far(kv_far), swap_mate(kv_mate),),
    )
    far_sums = call(
        functools.partial(sum_body, NEAR_SIZE),
        shape((NEAR_SIZE, ROWS, VARS_LANE), BF16),
        "vv", (along, joined),
    )
    everything = exchange(far_sums, NEAR)
    grad_wo, grad_dec = call(
        final_body,
        (shape((8, WIDTH), F32), shape((VARS, WIDTH), F32)),
        "svv", (band, everything, dec_weight,),
        scratch=[pltpu.VMEM((VARS_LANE, WIDTH), BF16), pltpu.VMEM((WO_ROWS, WIDTH), F32)],
    )
    return grad_states, grad_query, grad_key, grad_value, grad_wo, grad_dec


def solution(mesh):
    fine = Mesh(mesh.devices.reshape(SIZES), AXES)
    in_specs = (
        P(ENS, SPACE, None),
        P(ENS, SPACE, None),
        P(ENS, SPACE, None),
        P(ENS, SPACE, None),
        P(),
        P(),
        P(None, SPACE),
        P(SPACE),
        P(),
        P(None, SPACE),
        P(None, SPACE),
        P(None, SPACE),
    )
    out_specs = (
        P(ENS, SPACE, None),
        P(ENS, SPACE, None),
        P(ENS, SPACE, None),
        P(ENS, SPACE, None),
        P(SPACE, None),
        P(),
    )
    return jax.shard_map(
        per_device, mesh=fine, in_specs=in_specs, out_specs=out_specs, check_vma=False
    )
```

```python
import math

import jax
import jax.numpy as jnp
from jax import lax
from jax.experimental import pallas as pl
from jax.experimental.pallas import tpu as pltpu
from jax.sharding import Mesh
from jax.sharding import PartitionSpec as P

HEADS = 8
HEAD_DIM = 64
PAIR = 2 * HEAD_DIM
VARS = 100
VARS_SUB = 112
VARS_LANE = 128
MEMBERS = 8
NODES = 128
POINTS = 1024
SPAN = 3 * NODES
WIDTH = 1024
ATT = 512
SMOOTH_SQUARE = 0.0625
MASKED_SCORE = -1e30
SCALE = 1.0 / math.sqrt(HEAD_DIM)

AXES = ("zh", "y", "x", "zl", "c")
SIZES = (2, 4, 4, 8, 2)
ENS = ("zh", "y")
SPACE = ("x", "zl", "c")
NEAR = ("y", "x", "c")
NEAR_SIZE = 32
FAR = ("zh", "zl")
FAR_SIZE = 16
DEC_ROWS = WIDTH // NEAR_SIZE
WO_ROWS = ATT // NEAR_SIZE
ROWS = DEC_ROWS + WO_ROWS

WHOLE = 58 * 2**20
LONG = 2 * 10**10

F32 = jnp.float32
BF16 = jnp.bfloat16
NN = (((1,), (0,)), ((), ()))
NT = (((1,), (1,)), ((), ()))
TN = (((0,), (0,)), ((), ()))


def dot(a, b, dims):
    return lax.dot_general(a, b, dims, preferred_element_type=F32)


class Landing:
    def __init__(self, source, target, sem):
        self.target = target
        self.copy = pltpu.make_async_copy(source, target, sem)
        self.copy.start()

    def ready(self):
        self.copy.wait()
        return self.target


def call(body, out_shape, spaces, args, scratch=(), out_space=None, cost=10**8, limit=24 * 2**20):
    kinds = {
        "s": pl.BlockSpec(memory_space=pltpu.SMEM),
        "v": pl.BlockSpec(memory_space=pltpu.VMEM),
    }
    left = pl.BlockSpec(memory_space=pl.ANY)
    specs = [kinds.get(space, left) for space in spaces]
    landed = [i for i, space in enumerate(spaces) if space in "ltk"]
    outs = len(out_shape) if isinstance(out_shape, tuple) else 1
    if landed:
        targets = [
            pltpu.VMEM(args[i].shape if spaces[i] == "l" else (NODES, WIDTH), args[i].dtype)
            for i in landed
        ]
        scratch = [*targets, pltpu.SemaphoreType.DMA((len(landed),)), *scratch]

    def kernel(*refs):
        inputs = list(refs[: len(args)])
        results = refs[len(args) : len(args) + outs]
        rest = refs[len(args) + outs :]
        if landed:
            count = len(landed)
            for k, i in enumerate(landed):
                source = inputs[i]
                if spaces[i] == "t":
                    source = source.at[:, pl.ds(0, WIDTH)]
                if spaces[i] == "k":
                    source = source.at[:, pl.ds(WIDTH, WIDTH)]
                inputs[i] = Landing(source, rest[k], rest[count].at[k])
            rest = rest[count + 1 :]
        body(*inputs, *results, *rest)

    return pl.pallas_call(
        kernel,
        out_shape=out_shape,
        in_specs=specs,
        scratch_shapes=list(scratch),
        compiler_params=pltpu.CompilerParams(vmem_limit_bytes=limit),
        cost_estimate=pl.CostEstimate(flops=cost, bytes_accessed=10**6, transcendentals=0),
        **({} if out_space is None else {"out_specs": pl.BlockSpec(memory_space=out_space)}),
    )(*args)


def shape(dims, dtype):
    return jax.ShapeDtypeStruct(dims, dtype)


def smooth_slope(t):
    return t * lax.rsqrt(t * t + SMOOTH_SQUARE)


def split(x):
    high = x.astype(BF16)
    return high, (x - high.astype(F32)).astype(BF16)


def project_body(states_ref, dec_ref, proj_ref, pad_s):
    pad_s[...] = jnp.zeros(pad_s.shape, BF16)
    pad_s[0:VARS, :] = dec_ref.ready()[...]
    proj_ref[...] = dot(pad_s[...], states_ref.ready()[0], NT).astype(BF16)


def pack_body(states_hbm, key_hbm, value_hbm, after_ref, out_hbm, sems):
    copies = [
        pltpu.make_async_copy(states_hbm.at[0], out_hbm.at[:, pl.ds(0, WIDTH)], sems.at[0]),
        pltpu.make_async_copy(key_hbm.at[0], out_hbm.at[:, pl.ds(WIDTH, ATT)], sems.at[1]),
        pltpu.make_async_copy(value_hbm.at[0], out_hbm.at[:, pl.ds(WIDTH + ATT, ATT)], sems.at[2]),
    ]
    for copy in copies:
        copy.start()
    for copy in copies:
        copy.wait()


def pair_body(own_ref, other_ref, out_ref):
    own_ref, other_ref = own_ref.ready(), other_ref.ready()
    for i in range(out_ref.shape[0]):
        out_ref[i, 0:VARS_SUB, :] = own_ref[...]
        out_ref[i, VARS_SUB : 2 * VARS_SUB, :] = other_ref[...]


def bases(band):
    side = 2 * lax.rem(band, 2) - 1
    return (band + side) * NODES, band * NODES, (band - side) * NODES


def weights_body(band_ref, edges_ref, edge_weight_ref, area_ref, var_ref, mix_ref, weight_ref):
    edges = edges_ref[...]
    for part, base in enumerate(bases(band_ref[0])):
        place = lax.broadcasted_iota(jnp.int32, (NODES, POINTS), 0) + base
        mix = jnp.zeros((NODES, POINTS), F32)
        for slot in range(3):
            mix = mix + jnp.where(
                edges[slot : slot + 1, :] == place, edge_weight_ref[slot : slot + 1, :], 0.0
            )
        mix_ref[part * NODES : (part + 1) * NODES, :] = mix.astype(BF16)
    row = jnp.concatenate([var_ref[...], jnp.zeros((1, VARS_LANE - VARS), F32)], axis=1)
    column = jnp.transpose(jnp.broadcast_to(row, (VARS_LANE, VARS_LANE)))[0:VARS_SUB, 0:1]
    weight_ref[...] = column * area_ref[...]


def crps_body(
    member_ref,
    far_ref,
    mid_ref,
    mate_ref,
    mix_ref,
    weight_ref,
    target_ref,
    attn_ref,
    states_ref,
    far_states_ref,
    mate_states_ref,
    terms_ref,
    to_far_ref,
    own_ref,
    to_mate_ref,
    pred_s,
    grad_s,
):
    mix = mix_ref[...]
    for member in range(MEMBERS):
        rows = slice(member * VARS_SUB, (member + 1) * VARS_SUB)
        half = slice((member % 2) * VARS_SUB, (member % 2 + 1) * VARS_SUB)
        proj = jnp.concatenate([far_ref[rows], mid_ref[member // 2, half], mate_ref[rows]], axis=1)
        pred_s[member] = dot(proj, mix, NN)
    grad_s[...] = jnp.zeros(grad_s.shape, BF16)
    me = member_ref[0]
    for first in range(0, VARS, 16):
        rows = min(16, VARS - first)
        mine = pred_s[me, first : first + rows, :]
        total = jnp.zeros_like(mine)
        for member in range(MEMBERS):
            total = total + smooth_slope(mine - pred_s[member, first : first + rows, :])
        slopes = smooth_slope(mine - target_ref[first : first + rows, :]) - total * (
            1.0 / (MEMBERS - 1)
        )
        grad_s[first : first + rows, :] = (weight_ref[first : first + rows, :] * slopes).astype(
            BF16
        )
    grads = grad_s[...]
    sums = dot(mix, grads, NT)
    to_far_ref[...] = sums[0:NODES]
    own_ref[...] = sums[NODES : 2 * NODES]
    to_mate_ref[...] = sums[2 * NODES : SPAN]
    high, low = split(dot(grads, mix, NT))
    bands = (far_states_ref.ready(), states_ref.ready().at[0], mate_states_ref.ready())
    for block in range(WIDTH // NODES):
        cols = slice(block * NODES, (block + 1) * NODES)
        states = jnp.concatenate([band[:, cols] for band in bands], axis=0)
        dec = jnp.transpose(dot(high, states, NN) + dot(low, states, NN)).astype(BF16)
        count = NODES // DEC_ROWS
        terms_ref[block * count : (block + 1) * count, 0:DEC_ROWS, :] = dec.reshape(
            count, DEC_ROWS, VARS_LANE
        )
    attn_ref = attn_ref.ready()
    for block in range(ATT // PAIR):
        first = MEMBERS * VARS_SUB + block * NODES
        rows = slice(first, first + NODES)
        attn = jnp.concatenate([far_ref[rows], attn_ref[block], mate_ref[rows]], axis=0)
        wo = jnp.transpose(dot(high, attn, NN) + dot(low, attn, NN)).astype(BF16)
        count = NODES // WO_ROWS
        terms_ref[block * count : (block + 1) * count, DEC_ROWS:ROWS, :] = wo.reshape(
            count, WO_ROWS, VARS_LANE
        )


def sum_parts(in_ref, out_ref):
    total = in_ref[0].astype(F32)
    for i in range(1, in_ref.shape[0]):
        total = total + in_ref[i].astype(F32)
    total = total.astype(BF16)
    for i in range(out_ref.shape[0]):
        out_ref[i] = total


def near_body(in_ref, own_ref, far_ref, mate_ref, out_ref, total_ref):
    sum_parts(in_ref, out_ref)
    total_ref[...] = own_ref.ready()[...] + far_ref.ready()[...] + mate_ref.ready()[...]


def sum_body(in_ref, after_ref, out_ref):
    sum_parts(in_ref, out_ref)


def final_body(band_ref, all_ref, dec_ref, wo_ref, grad_dec_ref, done_ref, dec_s, wo_s):
    done_ref[...] = jnp.zeros(done_ref.shape, F32)
    dec_s[...] = jnp.zeros(dec_s.shape, BF16)
    dec_s[0:VARS, :] = dec_ref[...]
    band = band_ref[0]
    rows = all_ref[lax.div(band, 2), DEC_ROWS:ROWS, :]
    wo_s[...] = dot(rows, dec_s[...], NN)
    wo_ref[...] = wo_s[pl.ds(pl.multiple_of(lax.rem(band, 2) * 8, 8), 8), :]
    dec = all_ref[:, 0:DEC_ROWS, :].astype(F32).reshape(WIDTH, VARS_LANE)
    grad_dec_ref[...] = jnp.transpose(dec)[0:VARS, :]


def pair_masks(dtype):
    lane = lax.broadcasted_iota(jnp.int32, (1, PAIR), 1)
    return (lane < HEAD_DIM).astype(dtype), (lane >= HEAD_DIM).astype(dtype)


def band_blocks(far_ref, own_ref, mate_ref, pair, first):
    cols = slice(pair * PAIR, (pair + 1) * PAIR)
    side = slice(first + pair * PAIR, first + (pair + 1) * PAIR)
    return jnp.concatenate([far_ref[:, side], own_ref[0, :, cols], mate_ref[:, side]], axis=0)


def forward_body(
    band_ref, windows_ref, query_ref, key_ref, value_ref, far_ref, mate_ref, prob_ref, attn_ref
):
    query_ref, key_ref, value_ref = query_ref.ready(), key_ref.ready(), value_ref.ready()
    far_ref, mate_ref = far_ref.ready(), mate_ref.ready()
    lanes = lax.broadcasted_iota(jnp.int32, (1, NODES), 1)
    place = jnp.concatenate([lanes + base for base in bases(band_ref[0])], axis=1)
    inside = (place >= windows_ref[0, 0]) & (place < windows_ref[1, 0])
    masks = pair_masks(BF16)
    lane = lax.broadcasted_iota(jnp.int32, (1, PAIR), 1)
    for pair in range(HEADS // 2):
        cols = slice(pair * PAIR, (pair + 1) * PAIR)
        query = query_ref[0, :, cols]
        keys = band_blocks(far_ref, key_ref, mate_ref, pair, 0)
        values = band_blocks(far_ref, value_ref, mate_ref, pair, ATT)
        outs = []
        for half in range(2):
            scores = dot(query * masks[half], keys, NT) * SCALE
            scores = jnp.where(inside, scores, MASKED_SCORE)
            exponent = jnp.exp(scores - jnp.max(scores, axis=-1, keepdims=True))
            prob = exponent / jnp.sum(exponent, axis=-1, keepdims=True)
            prob_ref[2 * pair + half] = prob
            outs.append(dot(prob.astype(BF16), values, NN))
        attn_ref[pair] = jnp.where(lane < HEAD_DIM, outs[0], outs[1]).astype(BF16)


def backward_body(
    total_ref,
    dec_ref,
    out_weight_ref,
    query_ref,
    key_ref,
    value_ref,
    far_ref,
    mate_ref,
    prob_ref,
    after_ref,
    states_ref,
    grad_query_ref,
    to_far_ref,
    own_ref,
    to_mate_ref,
    done_ref,
    dec_s,
):
    done_ref[...] = jnp.zeros(done_ref.shape, F32)
    dec_s[...] = jnp.zeros(dec_s.shape, BF16)
    dec_s[0:VARS, :] = dec_ref.ready()[...]
    dec = dec_s[...]
    total = total_ref.ready()[...]
    grad_states = dot(
        jnp.concatenate(split(total), axis=1), jnp.concatenate([dec, dec], axis=0), NN
    ).astype(BF16)
    states_ref[0] = grad_states
    grad_out = dot(grad_states, out_weight_ref.ready()[...], NT).astype(BF16)
    query_ref, key_ref, value_ref = query_ref.ready(), key_ref.ready(), value_ref.ready()
    far_ref, mate_ref, prob_ref = far_ref.ready(), mate_ref.ready(), prob_ref.ready()
    masks = pair_masks(BF16)
    lane = lax.broadcasted_iota(jnp.int32, (1, PAIR), 1)
    first = lane < HEAD_DIM
    for pair in range(HEADS // 2):
        cols = slice(pair * PAIR, (pair + 1) * PAIR)
        vcols = slice(ATT + pair * PAIR, ATT + (pair + 1) * PAIR)
        query = query_ref[0, :, cols]
        keys = band_blocks(far_ref, key_ref, mate_ref, pair, 0)
        values = band_blocks(far_ref, value_ref, mate_ref, pair, ATT)
        grads = grad_out[:, cols]
        key_terms, value_terms, query_terms = [], [], []
        for half in range(2):
            prob = prob_ref[2 * pair + half]
            grad_prob = dot(grads * masks[half], values, NT)
            delta = jnp.sum(prob * grad_prob, axis=-1, keepdims=True)
            grad_scores = (prob * (grad_prob - delta)).astype(BF16)
            value_terms.append(dot(prob.astype(BF16), grads, TN))
            query_terms.append(dot(grad_scores, keys, NN))
            key_terms.append(dot(grad_scores, query, TN))
        grad_query_ref[0, :, cols] = (
            jnp.where(first, query_terms[0], query_terms[1]) * SCALE
        ).astype(BF16)
        key_term = jnp.where(first, key_terms[0], key_terms[1]) * SCALE
        value_term = jnp.where(first, value_terms[0], value_terms[1])
        for term, where in ((key_term, cols), (value_term, vcols)):
            to_far_ref[:, where] = term[0:NODES].astype(BF16)
            own_ref[:, where] = term[NODES : 2 * NODES]
            to_mate_ref[:, where] = term[2 * NODES : SPAN].astype(BF16)


def join_body(own_ref, far_ref, mate_ref, after_ref, key_ref, value_ref):
    own_ref, far_ref, mate_ref = own_ref.ready(), far_ref.ready(), mate_ref.ready()
    for first, ref in ((0, key_ref), (ATT, value_ref)):
        cols = slice(first, first + ATT)
        ref[0] = (
            own_ref[:, cols] + far_ref[:, cols].astype(F32) + mate_ref[:, cols].astype(F32)
        ).astype(BF16)


def swap_far(x):
    pairs = [(i, i + 1) for i in range(1, 63, 2)]
    return lax.ppermute(x, SPACE, pairs + [(target, source) for source, target in pairs])


def swap_mate(x):
    return lax.ppermute(x, "c", [(0, 1), (1, 0)])


def exchange(x, axes):
    return lax.all_to_all(x, axes, split_axis=0, concat_axis=0, tiled=True)


def per_device(
    node_states,
    query,
    key,
    value,
    out_weight,
    dec_weight,
    target,
    area_weight,
    var_weight,
    edges,
    edge_weight,
    windows,
):
    band = lax.axis_index(SPACE).astype(jnp.int32).reshape(1)
    member = (2 * lax.axis_index("y")).astype(jnp.int32).reshape(1)
    proj = call(
        project_body,
        shape((VARS_SUB, NODES), BF16),
        "ll",
        (node_states, dec_weight),
        scratch=[pltpu.VMEM((VARS_SUB, WIDTH), BF16)],
        limit=WHOLE,
    )
    other = lax.ppermute(proj, "zh", [(0, 1), (1, 0)])
    packed = call(
        pack_body,
        shape((NODES, 2 * WIDTH), BF16),
        "aaaa",
        (node_states, key, value, proj),
        scratch=[pltpu.SemaphoreType.DMA((3,))],
        out_space=pl.ANY,
        limit=WHOLE,
    )
    far_band, mate_band = swap_far(packed), swap_mate(packed)
    pairs = call(
        pair_body,
        shape((4, 2 * VARS_SUB, NODES), BF16),
        "ll",
        (proj, other),
        cost=LONG,
    )
    mid = exchange(pairs, "y")
    prob, attn = call(
        forward_body,
        (shape((HEADS, NODES, SPAN), F32), shape((ATT // PAIR, NODES, PAIR), BF16)),
        "sslllkk",
        (band, windows, query, key, value, far_band, mate_band),
    )
    mix, weight = call(
        weights_body,
        (shape((SPAN, POINTS), BF16), shape((VARS_SUB, POINTS), F32)),
        "svvvv",
        (band, edges, edge_weight, area_weight.reshape(1, -1), var_weight.reshape(1, -1)),
    )
    halo = jnp.concatenate([mid.reshape(-1, NODES), attn.reshape(-1, PAIR)], axis=0)
    block = shape((NODES, VARS_LANE), F32)
    terms, to_far, own, to_mate = call(
        crps_body,
        (shape((NEAR_SIZE, ROWS, VARS_LANE), BF16), block, block, block),
        "svvvvvvlltt",
        (
            member,
            swap_far(halo),
            mid,
            swap_mate(halo),
            mix,
            weight,
            target,
            attn,
            node_states,
            far_band,
            mate_band,
        ),
        scratch=[
            pltpu.VMEM((MEMBERS, VARS_SUB, POINTS), F32),
            pltpu.VMEM((VARS_LANE, POINTS), BF16),
        ],
    )
    near = exchange(terms, NEAR)
    near_sums, total = call(
        near_body,
        (shape((FAR_SIZE, ROWS, VARS_LANE), BF16), block),
        "vlll",
        (near, own, swap_far(to_far), swap_mate(to_mate)),
        cost=LONG,
    )
    along = exchange(near_sums, FAR)
    wide = (NODES, 2 * ATT)
    flag = shape((8, 128), F32)
    grad_states, grad_query, kv_far, kv_own, kv_mate, done = call(
        backward_body,
        (
            shape((1, NODES, WIDTH), BF16),
            shape((1, NODES, ATT), BF16),
            shape(wide, BF16),
            shape(wide, F32),
            shape(wide, BF16),
            flag,
        ),
        "llllllkkla",
        (
            total,
            dec_weight,
            out_weight,
            query,
            key,
            value,
            far_band,
            mate_band,
            prob,
            near_sums,
        ),
        scratch=[pltpu.VMEM((VARS_LANE, WIDTH), BF16)],
        limit=WHOLE,
    )
    far_sums = call(
        sum_body,
        shape((NEAR_SIZE, ROWS, VARS_LANE), BF16),
        "va",
        (along, done),
        cost=LONG,
    )
    everything = exchange(far_sums, NEAR)
    grad_wo, grad_dec, last = call(
        final_body,
        (shape((8, WIDTH), F32), shape((VARS, WIDTH), F32), flag),
        "svv",
        (band, everything, dec_weight),
        scratch=[pltpu.VMEM((VARS_LANE, WIDTH), BF16), pltpu.VMEM((WO_ROWS, WIDTH), F32)],
    )
    grad_key, grad_value = call(
        join_body,
        (shape((1, NODES, ATT), BF16), shape((1, NODES, ATT), BF16)),
        "llla",
        (kv_own, swap_far(kv_far), swap_mate(kv_mate), last),
    )
    return grad_states, grad_query, grad_key, grad_value, grad_wo, grad_dec


def solution(mesh):
    fine = Mesh(mesh.devices.reshape(SIZES), AXES)
    in_specs = (
        P(ENS, SPACE, None),
        P(ENS, SPACE, None),
        P(ENS, SPACE, None),
        P(ENS, SPACE, None),
        P(),
        P(),
        P(None, SPACE),
        P(SPACE),
        P(),
        P(None, SPACE),
        P(None, SPACE),
        P(None, SPACE),
    )
    out_specs = (
        P(ENS, SPACE, None),
        P(ENS, SPACE, None),
        P(ENS, SPACE, None),
        P(ENS, SPACE, None),
        P(SPACE, None),
        P(),
    )
    return jax.shard_map(
        per_device, mesh=fine, in_specs=in_specs, out_specs=out_specs, check_vma=False
    )
```

```python
import math

import jax
import jax.numpy as jnp
from jax import lax
from jax.experimental import pallas as pl
from jax.experimental.pallas import tpu as pltpu
from jax.sharding import Mesh
from jax.sharding import PartitionSpec as P

HEADS = 8
HEAD_DIM = 64
PAIR = 2 * HEAD_DIM
VARS = 100
VARS_SUB = 112
VARS_LANE = 128
MEMBERS = 8
NODES = 128
POINTS = 1024
SPAN = 3 * NODES
WIDTH = 1024
ATT = 512
SMOOTH_SQUARE = 0.0625
MASKED_SCORE = -1e30
SCALE = 1.0 / math.sqrt(HEAD_DIM)

AXES = ("zh", "y", "x", "zl", "c")
SIZES = (2, 4, 4, 8, 2)
ENS = ("zh", "y")
SPACE = ("x", "zl", "c")
NEAR = ("y", "x", "c")
NEAR_SIZE = 32
FAR = ("zh", "zl")
FAR_SIZE = 16
DEC_ROWS = WIDTH // NEAR_SIZE
WO_ROWS = ATT // NEAR_SIZE
ROWS = DEC_ROWS + WO_ROWS

WHOLE = 58 * 2**20
LONG = 2 * 10**10

F32 = jnp.float32
BF16 = jnp.bfloat16
NN = (((1,), (0,)), ((), ()))
NT = (((1,), (1,)), ((), ()))
TN = (((0,), (0,)), ((), ()))


def dot(a, b, dims):
    return lax.dot_general(a, b, dims, preferred_element_type=F32)


class Landing:
    def __init__(self, source, target, sem):
        self.target = target
        self.copy = pltpu.make_async_copy(source, target, sem)
        self.copy.start()

    def ready(self):
        self.copy.wait()
        return self.target


def call(body, out_shape, spaces, args, scratch=(), cost=10**8, limit=24 * 2**20):
    kinds = {
        "s": pl.BlockSpec(memory_space=pltpu.SMEM),
        "v": pl.BlockSpec(memory_space=pltpu.VMEM),
    }
    left = pl.BlockSpec(memory_space=pl.ANY)
    specs = [kinds.get(space, left) for space in spaces]
    landed = [i for i, space in enumerate(spaces) if space in "ltk"]
    outs = len(out_shape) if isinstance(out_shape, tuple) else 1
    if landed:
        targets = [
            pltpu.VMEM(args[i].shape if spaces[i] == "l" else (NODES, WIDTH), args[i].dtype)
            for i in landed
        ]
        scratch = [*targets, pltpu.SemaphoreType.DMA((len(landed),)), *scratch]

    def kernel(*refs):
        inputs = list(refs[: len(args)])
        results = refs[len(args) : len(args) + outs]
        rest = refs[len(args) + outs :]
        if landed:
            count = len(landed)
            for k, i in enumerate(landed):
                source = inputs[i]
                if spaces[i] == "t":
                    source = source.at[:, pl.ds(0, WIDTH)]
                if spaces[i] == "k":
                    source = source.at[:, pl.ds(WIDTH, WIDTH)]
                inputs[i] = Landing(source, rest[k], rest[count].at[k])
            rest = rest[count + 1 :]
        body(*inputs, *results, *rest)

    return pl.pallas_call(
        kernel,
        out_shape=out_shape,
        in_specs=specs,
        scratch_shapes=list(scratch),
        compiler_params=pltpu.CompilerParams(vmem_limit_bytes=limit),
        cost_estimate=pl.CostEstimate(flops=cost, bytes_accessed=10**6, transcendentals=0),
    )(*args)


def shape(dims, dtype):
    return jax.ShapeDtypeStruct(dims, dtype)


def smooth_slope(t):
    return t * lax.rsqrt(t * t + SMOOTH_SQUARE)


def split(x):
    high = x.astype(BF16)
    return high, (x - high.astype(F32)).astype(BF16)


def project_body(states_ref, dec_ref, proj_ref, pad_s):
    pad_s[...] = jnp.zeros(pad_s.shape, BF16)
    pad_s[0:VARS, :] = dec_ref.ready()[...]
    proj_ref[...] = dot(pad_s[...], states_ref.ready()[0], NT).astype(BF16)


def pack_body(states_hbm, key_hbm, value_hbm, after_ref, out_ref, sems):
    copies = [
        pltpu.make_async_copy(states_hbm.at[0], out_ref.at[:, pl.ds(0, WIDTH)], sems.at[0]),
        pltpu.make_async_copy(key_hbm.at[0], out_ref.at[:, pl.ds(WIDTH, ATT)], sems.at[1]),
        pltpu.make_async_copy(value_hbm.at[0], out_ref.at[:, pl.ds(WIDTH + ATT, ATT)], sems.at[2]),
    ]
    for copy in copies:
        copy.start()
    for copy in copies:
        copy.wait()


def pair_body(own_ref, other_ref, out_ref):
    own_ref, other_ref = own_ref.ready(), other_ref.ready()
    for i in range(out_ref.shape[0]):
        out_ref[i, 0:VARS_SUB, :] = own_ref[...]
        out_ref[i, VARS_SUB : 2 * VARS_SUB, :] = other_ref[...]


def bases(band):
    side = 2 * lax.rem(band, 2) - 1
    return (band + side) * NODES, band * NODES, (band - side) * NODES


def weights_body(band_ref, edges_ref, edge_weight_ref, area_ref, var_ref, mix_ref, weight_ref):
    edges = edges_ref[...]
    for part, base in enumerate(bases(band_ref[0])):
        place = lax.broadcasted_iota(jnp.int32, (NODES, POINTS), 0) + base
        mix = jnp.zeros((NODES, POINTS), F32)
        for slot in range(3):
            mix = mix + jnp.where(
                edges[slot : slot + 1, :] == place, edge_weight_ref[slot : slot + 1, :], 0.0
            )
        mix_ref[part * NODES : (part + 1) * NODES, :] = mix.astype(BF16)
    row = jnp.concatenate([var_ref[...], jnp.zeros((1, VARS_LANE - VARS), F32)], axis=1)
    column = jnp.transpose(jnp.broadcast_to(row, (VARS_LANE, VARS_LANE)))[0:VARS_SUB, 0:1]
    weight_ref[...] = column * area_ref[...]


def crps_body(
    member_ref,
    far_ref,
    mid_ref,
    mate_ref,
    mix_ref,
    weight_ref,
    target_ref,
    attn_ref,
    states_ref,
    far_states_ref,
    mate_states_ref,
    terms_ref,
    to_far_ref,
    own_ref,
    to_mate_ref,
    pred_s,
    grad_s,
):
    mix = mix_ref[...]
    for member in range(MEMBERS):
        rows = slice(member * VARS_SUB, (member + 1) * VARS_SUB)
        half = slice((member % 2) * VARS_SUB, (member % 2 + 1) * VARS_SUB)
        proj = jnp.concatenate([far_ref[rows], mid_ref[member // 2, half], mate_ref[rows]], axis=1)
        pred_s[member] = dot(proj, mix, NN)
    grad_s[...] = jnp.zeros(grad_s.shape, BF16)
    me = member_ref[0]
    for first in range(0, VARS, 16):
        rows = min(16, VARS - first)
        mine = pred_s[me, first : first + rows, :]
        total = jnp.zeros_like(mine)
        for member in range(MEMBERS):
            total = total + smooth_slope(mine - pred_s[member, first : first + rows, :])
        slopes = smooth_slope(mine - target_ref[first : first + rows, :]) - total * (
            1.0 / (MEMBERS - 1)
        )
        grad_s[first : first + rows, :] = (weight_ref[first : first + rows, :] * slopes).astype(
            BF16
        )
    grads = grad_s[...]
    sums = dot(mix, grads, NT)
    to_far_ref[...] = sums[0:NODES]
    own_ref[...] = sums[NODES : 2 * NODES]
    to_mate_ref[...] = sums[2 * NODES : SPAN]
    high, low = split(dot(grads, mix, NT))
    bands = (far_states_ref.ready(), states_ref.ready().at[0], mate_states_ref.ready())
    for block in range(WIDTH // NODES):
        cols = slice(block * NODES, (block + 1) * NODES)
        states = jnp.concatenate([band[:, cols] for band in bands], axis=0)
        dec = jnp.transpose(dot(high, states, NN) + dot(low, states, NN)).astype(BF16)
        count = NODES // DEC_ROWS
        terms_ref[block * count : (block + 1) * count, 0:DEC_ROWS, :] = dec.reshape(
            count, DEC_ROWS, VARS_LANE
        )
    attn_ref = attn_ref.ready()
    for block in range(ATT // PAIR):
        first = MEMBERS * VARS_SUB + block * NODES
        rows = slice(first, first + NODES)
        attn = jnp.concatenate([far_ref[rows], attn_ref[block], mate_ref[rows]], axis=0)
        wo = jnp.transpose(dot(high, attn, NN) + dot(low, attn, NN)).astype(BF16)
        count = NODES // WO_ROWS
        terms_ref[block * count : (block + 1) * count, DEC_ROWS:ROWS, :] = wo.reshape(
            count, WO_ROWS, VARS_LANE
        )


def sum_parts(in_ref, out_ref):
    total = in_ref[0].astype(F32)
    for i in range(1, in_ref.shape[0]):
        total = total + in_ref[i].astype(F32)
    total = total.astype(BF16)
    for i in range(out_ref.shape[0]):
        out_ref[i] = total


def near_body(in_ref, out_ref):
    sum_parts(in_ref, out_ref)


def sum_body(in_ref, after_ref, out_ref):
    sum_parts(in_ref, out_ref)


def final_body(band_ref, all_ref, dec_ref, after_ref, wo_ref, grad_dec_ref, dec_s, wo_s):
    dec_s[...] = jnp.zeros(dec_s.shape, BF16)
    dec_s[0:VARS, :] = dec_ref[...]
    band = band_ref[0]
    rows = all_ref[lax.div(band, 2), DEC_ROWS:ROWS, :]
    wo_s[...] = dot(rows, dec_s[...], NN)
    wo_ref[...] = wo_s[pl.ds(pl.multiple_of(lax.rem(band, 2) * 8, 8), 8), :]
    dec = all_ref[:, 0:DEC_ROWS, :].astype(F32).reshape(WIDTH, VARS_LANE)
    grad_dec_ref[...] = jnp.transpose(dec)[0:VARS, :]


def pair_masks(dtype):
    lane = lax.broadcasted_iota(jnp.int32, (1, PAIR), 1)
    return (lane < HEAD_DIM).astype(dtype), (lane >= HEAD_DIM).astype(dtype)


def band_blocks(far_ref, own_ref, mate_ref, pair, first):
    cols = slice(pair * PAIR, (pair + 1) * PAIR)
    side = slice(first + pair * PAIR, first + (pair + 1) * PAIR)
    return jnp.concatenate([far_ref[:, side], own_ref[0, :, cols], mate_ref[:, side]], axis=0)


def forward_body(
    band_ref, windows_ref, query_ref, key_ref, value_ref, far_ref, mate_ref, prob_ref, attn_ref
):
    query_ref, key_ref, value_ref = query_ref.ready(), key_ref.ready(), value_ref.ready()
    far_ref, mate_ref = far_ref.ready(), mate_ref.ready()
    lanes = lax.broadcasted_iota(jnp.int32, (1, NODES), 1)
    place = jnp.concatenate([lanes + base for base in bases(band_ref[0])], axis=1)
    inside = (place >= windows_ref[0, 0]) & (place < windows_ref[1, 0])
    masks = pair_masks(BF16)
    lane = lax.broadcasted_iota(jnp.int32, (1, PAIR), 1)
    for pair in range(HEADS // 2):
        cols = slice(pair * PAIR, (pair + 1) * PAIR)
        query = query_ref[0, :, cols]
        keys = band_blocks(far_ref, key_ref, mate_ref, pair, 0)
        values = band_blocks(far_ref, value_ref, mate_ref, pair, ATT)
        outs = []
        for half in range(2):
            scores = dot(query * masks[half], keys, NT) * SCALE
            scores = jnp.where(inside, scores, MASKED_SCORE)
            exponent = jnp.exp(scores - jnp.max(scores, axis=-1, keepdims=True))
            prob = exponent / jnp.sum(exponent, axis=-1, keepdims=True)
            prob_ref[2 * pair + half] = prob
            outs.append(dot(prob.astype(BF16), values, NN))
        attn_ref[pair] = jnp.where(lane < HEAD_DIM, outs[0], outs[1]).astype(BF16)


def backward_body(
    own_sum_ref,
    far_sum_ref,
    mate_sum_ref,
    dec_ref,
    out_weight_ref,
    query_ref,
    key_ref,
    value_ref,
    far_ref,
    mate_ref,
    prob_ref,
    after_ref,
    states_ref,
    grad_query_ref,
    to_far_ref,
    own_ref,
    to_mate_ref,
    done_ref,
    dec_s,
):
    done_ref[...] = jnp.zeros(done_ref.shape, F32)
    dec_s[...] = jnp.zeros(dec_s.shape, BF16)
    dec_s[0:VARS, :] = dec_ref.ready()[...]
    dec = dec_s[...]
    total = own_sum_ref.ready()[...] + far_sum_ref.ready()[...] + mate_sum_ref.ready()[...]
    grad_states = dot(
        jnp.concatenate(split(total), axis=1), jnp.concatenate([dec, dec], axis=0), NN
    ).astype(BF16)
    states_ref[0] = grad_states
    grad_out = dot(grad_states, out_weight_ref.ready()[...], NT).astype(BF16)
    query_ref, key_ref, value_ref = query_ref.ready(), key_ref.ready(), value_ref.ready()
    far_ref, mate_ref, prob_ref = far_ref.ready(), mate_ref.ready(), prob_ref.ready()
    masks = pair_masks(BF16)
    lane = lax.broadcasted_iota(jnp.int32, (1, PAIR), 1)
    first = lane < HEAD_DIM
    for pair in range(HEADS // 2):
        cols = slice(pair * PAIR, (pair + 1) * PAIR)
        vcols = slice(ATT + pair * PAIR, ATT + (pair + 1) * PAIR)
        query = query_ref[0, :, cols]
        keys = band_blocks(far_ref, key_ref, mate_ref, pair, 0)
        values = band_blocks(far_ref, value_ref, mate_ref, pair, ATT)
        grads = grad_out[:, cols]
        key_terms, value_terms, query_terms = [], [], []
        for half in range(2):
            prob = prob_ref[2 * pair + half]
            grad_prob = dot(grads * masks[half], values, NT)
            delta = jnp.sum(prob * grad_prob, axis=-1, keepdims=True)
            grad_scores = (prob * (grad_prob - delta)).astype(BF16)
            value_terms.append(dot(prob.astype(BF16), grads, TN))
            query_terms.append(dot(grad_scores, keys, NN))
            key_terms.append(dot(grad_scores, query, TN))
        grad_query_ref[0, :, cols] = (
            jnp.where(first, query_terms[0], query_terms[1]) * SCALE
        ).astype(BF16)
        key_term = jnp.where(first, key_terms[0], key_terms[1]) * SCALE
        value_term = jnp.where(first, value_terms[0], value_terms[1])
        for term, where in ((key_term, cols), (value_term, vcols)):
            to_far_ref[:, where] = term[0:NODES].astype(BF16)
            own_ref[:, where] = term[NODES : 2 * NODES]
            to_mate_ref[:, where] = term[2 * NODES : SPAN].astype(BF16)


def join_body(own_ref, far_ref, mate_ref, key_ref, value_ref, done_ref):
    done_ref[...] = jnp.zeros(done_ref.shape, F32)
    own_ref, far_ref, mate_ref = own_ref.ready(), far_ref.ready(), mate_ref.ready()
    for first, ref in ((0, key_ref), (ATT, value_ref)):
        cols = slice(first, first + ATT)
        ref[0] = (
            own_ref[:, cols] + far_ref[:, cols].astype(F32) + mate_ref[:, cols].astype(F32)
        ).astype(BF16)


def swap_far(x):
    pairs = [(i, i + 1) for i in range(1, 63, 2)]
    return lax.ppermute(x, SPACE, pairs + [(target, source) for source, target in pairs])


def swap_mate(x):
    return lax.ppermute(x, "c", [(0, 1), (1, 0)])


def exchange(x, axes):
    return lax.all_to_all(x, axes, split_axis=0, concat_axis=0, tiled=True)


def per_device(
    node_states,
    query,
    key,
    value,
    out_weight,
    dec_weight,
    target,
    area_weight,
    var_weight,
    edges,
    edge_weight,
    windows,
):
    band = lax.axis_index(SPACE).astype(jnp.int32).reshape(1)
    member = (2 * lax.axis_index("y")).astype(jnp.int32).reshape(1)
    proj = call(
        project_body,
        shape((VARS_SUB, NODES), BF16),
        "ll",
        (node_states, dec_weight),
        scratch=[pltpu.VMEM((VARS_SUB, WIDTH), BF16)],
        limit=WHOLE,
    )
    other = lax.ppermute(proj, "zh", [(0, 1), (1, 0)])
    packed = call(
        pack_body,
        shape((NODES, 2 * WIDTH), BF16),
        "aaaa",
        (node_states, key, value, proj),
        scratch=[pltpu.SemaphoreType.DMA((3,))],
        limit=WHOLE,
    )
    mate_band, far_band = swap_mate(packed), swap_far(packed)
    pairs = call(
        pair_body,
        shape((4, 2 * VARS_SUB, NODES), BF16),
        "ll",
        (proj, other),
        cost=LONG,
    )
    mid = exchange(pairs, "y")
    prob, attn = call(
        forward_body,
        (shape((HEADS, NODES, SPAN), F32), shape((ATT // PAIR, NODES, PAIR), BF16)),
        "sslllkk",
        (band, windows, query, key, value, far_band, mate_band),
    )
    mix, weight = call(
        weights_body,
        (shape((SPAN, POINTS), BF16), shape((VARS_SUB, POINTS), F32)),
        "svvvv",
        (band, edges, edge_weight, area_weight.reshape(1, -1), var_weight.reshape(1, -1)),
    )
    halo = jnp.concatenate([mid.reshape(-1, NODES), attn.reshape(-1, PAIR)], axis=0)
    mate_halo, far_halo = swap_mate(halo), swap_far(halo)
    block = shape((NODES, VARS_LANE), F32)
    terms, to_far, own, to_mate = call(
        crps_body,
        (shape((NEAR_SIZE, ROWS, VARS_LANE), BF16), block, block, block),
        "svvvvvvlltt",
        (
            member,
            far_halo,
            mid,
            mate_halo,
            mix,
            weight,
            target,
            attn,
            node_states,
            far_band,
            mate_band,
        ),
        scratch=[
            pltpu.VMEM((MEMBERS, VARS_SUB, POINTS), F32),
            pltpu.VMEM((VARS_LANE, POINTS), BF16),
        ],
    )
    near = exchange(terms, NEAR)
    mate_sum, far_sum = swap_mate(to_mate), swap_far(to_far)
    near_sums = call(
        near_body, shape((FAR_SIZE, ROWS, VARS_LANE), BF16), "v", (near,), cost=LONG
    )
    along = exchange(near_sums, FAR)
    wide = (NODES, 2 * ATT)
    flag = shape((8, 128), F32)
    grad_states, grad_query, kv_far, kv_own, kv_mate, done = call(
        backward_body,
        (
            shape((1, NODES, WIDTH), BF16),
            shape((1, NODES, ATT), BF16),
            shape(wide, BF16),
            shape(wide, F32),
            shape(wide, BF16),
            flag,
        ),
        "llllllllkkla",
        (
            own,
            far_sum,
            mate_sum,
            dec_weight,
            out_weight,
            query,
            key,
            value,
            far_band,
            mate_band,
            prob,
            near_sums,
        ),
        scratch=[pltpu.VMEM((VARS_LANE, WIDTH), BF16)],
        limit=WHOLE,
        cost=LONG,
    )
    far_sums = call(
        sum_body,
        shape((NEAR_SIZE, ROWS, VARS_LANE), BF16),
        "va",
        (along, done),
        cost=LONG,
    )
    everything = exchange(far_sums, NEAR)
    mate_term, far_term = swap_mate(kv_mate), swap_far(kv_far)
    grad_key, grad_value, joined = call(
        join_body,
        (shape((1, NODES, ATT), BF16), shape((1, NODES, ATT), BF16), flag),
        "lll",
        (kv_own, far_term, mate_term),
        cost=LONG,
    )
    grad_wo, grad_dec = call(
        final_body,
        (shape((8, WIDTH), F32), shape((VARS, WIDTH), F32)),
        "svva",
        (band, everything, dec_weight, joined),
        scratch=[pltpu.VMEM((VARS_LANE, WIDTH), BF16), pltpu.VMEM((WO_ROWS, WIDTH), F32)],
    )
    return grad_states, grad_query, grad_key, grad_value, grad_wo, grad_dec


def solution(mesh):
    fine = Mesh(mesh.devices.reshape(SIZES), AXES)
    in_specs = (
        P(ENS, SPACE, None),
        P(ENS, SPACE, None),
        P(ENS, SPACE, None),
        P(ENS, SPACE, None),
        P(),
        P(),
        P(None, SPACE),
        P(SPACE),
        P(),
        P(None, SPACE),
        P(None, SPACE),
        P(None, SPACE),
    )
    out_specs = (
        P(ENS, SPACE, None),
        P(ENS, SPACE, None),
        P(ENS, SPACE, None),
        P(ENS, SPACE, None),
        P(SPACE, None),
        P(),
    )
    return jax.shard_map(
        per_device, mesh=fine, in_specs=in_specs, out_specs=out_specs, check_vma=False
    )
```

```python
import math

import jax
import jax.numpy as jnp
from jax import lax
from jax.experimental import pallas as pl
from jax.experimental.pallas import tpu as pltpu
from jax.sharding import Mesh
from jax.sharding import PartitionSpec as P

HEADS = 8
HEAD_DIM = 64
PAIR = 2 * HEAD_DIM
VARS = 100
VARS_SUB = 112
VARS_LANE = 128
MEMBERS = 8
NODES = 128
POINTS = 1024
SPAN = 3 * NODES
WIDTH = 1024
ATT = 512
SMOOTH_SQUARE = 0.0625
MASKED_SCORE = -1e30
SCALE = 1.0 / math.sqrt(HEAD_DIM)

AXES = ("zh", "y", "x", "zl", "c")
SIZES = (2, 4, 4, 8, 2)
ENS = ("zh", "y")
SPACE = ("x", "zl", "c")
NEAR = ("y", "x", "c")
NEAR_SIZE = 32
FAR = ("zh", "zl")
FAR_SIZE = 16
DEC_ROWS = WIDTH // NEAR_SIZE
WO_ROWS = ATT // NEAR_SIZE
ROWS = DEC_ROWS + WO_ROWS

WHOLE = 58 * 2**20
LONG = 2 * 10**10

F32 = jnp.float32
BF16 = jnp.bfloat16
NN = (((1,), (0,)), ((), ()))
NT = (((1,), (1,)), ((), ()))
TN = (((0,), (0,)), ((), ()))


def dot(a, b, dims):
    return lax.dot_general(a, b, dims, preferred_element_type=F32)


class Landing:
    def __init__(self, source, target, sem):
        self.target = target
        self.copy = pltpu.make_async_copy(source, target, sem)
        self.copy.start()

    def ready(self):
        self.copy.wait()
        return self.target


def call(body, out_shape, spaces, args, scratch=(), cost=10**8, limit=24 * 2**20):
    kinds = {
        "s": pl.BlockSpec(memory_space=pltpu.SMEM),
        "v": pl.BlockSpec(memory_space=pltpu.VMEM),
    }
    left = pl.BlockSpec(memory_space=pl.ANY)
    specs = [kinds.get(space, left) for space in spaces]
    landed = [i for i, space in enumerate(spaces) if space in "ltk"]
    outs = len(out_shape) if isinstance(out_shape, tuple) else 1
    if landed:
        targets = [
            pltpu.VMEM(args[i].shape if spaces[i] == "l" else (NODES, WIDTH), args[i].dtype)
            for i in landed
        ]
        scratch = [*targets, pltpu.SemaphoreType.DMA((len(landed),)), *scratch]

    def kernel(*refs):
        inputs = list(refs[: len(args)])
        results = refs[len(args) : len(args) + outs]
        rest = refs[len(args) + outs :]
        if landed:
            count = len(landed)
            for k, i in enumerate(landed):
                source = inputs[i]
                if spaces[i] == "t":
                    source = source.at[:, pl.ds(0, WIDTH)]
                if spaces[i] == "k":
                    source = source.at[:, pl.ds(WIDTH, WIDTH)]
                inputs[i] = Landing(source, rest[k], rest[count].at[k])
            rest = rest[count + 1 :]
        body(*inputs, *results, *rest)

    return pl.pallas_call(
        kernel,
        out_shape=out_shape,
        in_specs=specs,
        scratch_shapes=list(scratch),
        compiler_params=pltpu.CompilerParams(vmem_limit_bytes=limit),
        cost_estimate=pl.CostEstimate(flops=cost, bytes_accessed=10**6, transcendentals=0),
    )(*args)


def shape(dims, dtype):
    return jax.ShapeDtypeStruct(dims, dtype)


def smooth_slope(t):
    return t * lax.rsqrt(t * t + SMOOTH_SQUARE)


def split(x):
    high = x.astype(BF16)
    return high, (x - high.astype(F32)).astype(BF16)


def project_body(states_ref, dec_ref, proj_ref, pad_s):
    pad_s[...] = jnp.zeros(pad_s.shape, BF16)
    pad_s[0:VARS, :] = dec_ref.ready()[...]
    proj_ref[...] = dot(pad_s[...], states_ref.ready()[0], NT).astype(BF16)


def pack_body(states_hbm, key_hbm, value_hbm, after_ref, out_ref, sems):
    copies = [
        pltpu.make_async_copy(states_hbm.at[0], out_ref.at[:, pl.ds(0, WIDTH)], sems.at[0]),
        pltpu.make_async_copy(key_hbm.at[0], out_ref.at[:, pl.ds(WIDTH, ATT)], sems.at[1]),
        pltpu.make_async_copy(value_hbm.at[0], out_ref.at[:, pl.ds(WIDTH + ATT, ATT)], sems.at[2]),
    ]
    for copy in copies:
        copy.start()
    for copy in copies:
        copy.wait()


def pair_body(own_ref, other_ref, out_ref):
    own_ref, other_ref = own_ref.ready(), other_ref.ready()
    for i in range(out_ref.shape[0]):
        out_ref[i, 0:VARS_SUB, :] = own_ref[...]
        out_ref[i, VARS_SUB : 2 * VARS_SUB, :] = other_ref[...]


def bases(band):
    side = 2 * lax.rem(band, 2) - 1
    return (band + side) * NODES, band * NODES, (band - side) * NODES


def weights_body(band_ref, edges_ref, edge_weight_ref, area_ref, var_ref, mix_ref, weight_ref):
    edges = edges_ref[...]
    for part, base in enumerate(bases(band_ref[0])):
        place = lax.broadcasted_iota(jnp.int32, (NODES, POINTS), 0) + base
        mix = jnp.zeros((NODES, POINTS), F32)
        for slot in range(3):
            mix = mix + jnp.where(
                edges[slot : slot + 1, :] == place, edge_weight_ref[slot : slot + 1, :], 0.0
            )
        mix_ref[part * NODES : (part + 1) * NODES, :] = mix.astype(BF16)
    row = jnp.concatenate([var_ref[...], jnp.zeros((1, VARS_LANE - VARS), F32)], axis=1)
    column = jnp.transpose(jnp.broadcast_to(row, (VARS_LANE, VARS_LANE)))[0:VARS_SUB, 0:1]
    weight_ref[...] = column * area_ref[...]


def crps_body(
    member_ref,
    mate_ref,
    mid_ref,
    far_ref,
    mix_ref,
    weight_ref,
    target_ref,
    attn_ref,
    states_ref,
    mate_states_ref,
    far_states_ref,
    terms_ref,
    to_far_ref,
    own_ref,
    to_mate_ref,
    pred_s,
    grad_s,
):
    mix = mix_ref[...]
    for member in range(MEMBERS):
        rows = slice(member * VARS_SUB, (member + 1) * VARS_SUB)
        half = slice((member % 2) * VARS_SUB, (member % 2 + 1) * VARS_SUB)
        proj = jnp.concatenate([far_ref[rows], mid_ref[member // 2, half], mate_ref[rows]], axis=1)
        pred_s[member] = dot(proj, mix, NN)
    grad_s[...] = jnp.zeros(grad_s.shape, BF16)
    me = member_ref[0]
    for first in range(0, VARS, 16):
        rows = min(16, VARS - first)
        mine = pred_s[me, first : first + rows, :]
        total = jnp.zeros_like(mine)
        for member in range(MEMBERS):
            total = total + smooth_slope(mine - pred_s[member, first : first + rows, :])
        slopes = smooth_slope(mine - target_ref[first : first + rows, :]) - total * (
            1.0 / (MEMBERS - 1)
        )
        grad_s[first : first + rows, :] = (weight_ref[first : first + rows, :] * slopes).astype(
            BF16
        )
    grads = grad_s[...]
    sums = dot(mix, grads, NT)
    to_far_ref[...] = sums[0:NODES]
    own_ref[...] = sums[NODES : 2 * NODES]
    to_mate_ref[...] = sums[2 * NODES : SPAN]
    high, low = split(dot(grads, mix, NT))
    bands = (far_states_ref.ready(), states_ref.ready().at[0], mate_states_ref.ready())
    for block in range(WIDTH // NODES):
        cols = slice(block * NODES, (block + 1) * NODES)
        states = jnp.concatenate([band[:, cols] for band in bands], axis=0)
        dec = jnp.transpose(dot(high, states, NN) + dot(low, states, NN)).astype(BF16)
        count = NODES // DEC_ROWS
        terms_ref[block * count : (block + 1) * count, 0:DEC_ROWS, :] = dec.reshape(
            count, DEC_ROWS, VARS_LANE
        )
    attn_ref = attn_ref.ready()
    for block in range(ATT // PAIR):
        first = MEMBERS * VARS_SUB + block * NODES
        rows = slice(first, first + NODES)
        attn = jnp.concatenate([far_ref[rows], attn_ref[block], mate_ref[rows]], axis=0)
        wo = jnp.transpose(dot(high, attn, NN) + dot(low, attn, NN)).astype(BF16)
        count = NODES // WO_ROWS
        terms_ref[block * count : (block + 1) * count, DEC_ROWS:ROWS, :] = wo.reshape(
            count, WO_ROWS, VARS_LANE
        )


def sum_parts(in_ref, out_ref):
    total = in_ref[0].astype(F32)
    for i in range(1, in_ref.shape[0]):
        total = total + in_ref[i].astype(F32)
    total = total.astype(BF16)
    for i in range(out_ref.shape[0]):
        out_ref[i] = total


def near_body(in_ref, out_ref):
    sum_parts(in_ref, out_ref)


def sum_body(in_ref, out_ref):
    sum_parts(in_ref, out_ref)


def final_body(band_ref, all_ref, dec_ref, after_ref, wo_ref, grad_dec_ref, dec_s, wo_s):
    dec_s[...] = jnp.zeros(dec_s.shape, BF16)
    dec_s[0:VARS, :] = dec_ref[...]
    band = band_ref[0]
    rows = all_ref[lax.div(band, 2), DEC_ROWS:ROWS, :]
    wo_s[...] = dot(rows, dec_s[...], NN)
    wo_ref[...] = wo_s[pl.ds(pl.multiple_of(lax.rem(band, 2) * 8, 8), 8), :]
    dec = all_ref[:, 0:DEC_ROWS, :].astype(F32).reshape(WIDTH, VARS_LANE)
    grad_dec_ref[...] = jnp.transpose(dec)[0:VARS, :]


def pair_masks(dtype):
    lane = lax.broadcasted_iota(jnp.int32, (1, PAIR), 1)
    return (lane < HEAD_DIM).astype(dtype), (lane >= HEAD_DIM).astype(dtype)


def band_blocks(far_ref, own_ref, mate_ref, pair, first):
    cols = slice(pair * PAIR, (pair + 1) * PAIR)
    side = slice(first + pair * PAIR, first + (pair + 1) * PAIR)
    return jnp.concatenate([far_ref[:, side], own_ref[0, :, cols], mate_ref[:, side]], axis=0)


def forward_body(
    band_ref, windows_ref, query_ref, key_ref, value_ref, mate_ref, far_ref, prob_ref, attn_ref
):
    query_ref, key_ref, value_ref = query_ref.ready(), key_ref.ready(), value_ref.ready()
    far_ref, mate_ref = far_ref.ready(), mate_ref.ready()
    lanes = lax.broadcasted_iota(jnp.int32, (1, NODES), 1)
    place = jnp.concatenate([lanes + base for base in bases(band_ref[0])], axis=1)
    inside = (place >= windows_ref[0, 0]) & (place < windows_ref[1, 0])
    masks = pair_masks(BF16)
    lane = lax.broadcasted_iota(jnp.int32, (1, PAIR), 1)
    for pair in range(HEADS // 2):
        cols = slice(pair * PAIR, (pair + 1) * PAIR)
        query = query_ref[0, :, cols]
        keys = band_blocks(far_ref, key_ref, mate_ref, pair, 0)
        values = band_blocks(far_ref, value_ref, mate_ref, pair, ATT)
        outs = []
        for half in range(2):
            scores = dot(query * masks[half], keys, NT) * SCALE
            scores = jnp.where(inside, scores, MASKED_SCORE)
            exponent = jnp.exp(scores - jnp.max(scores, axis=-1, keepdims=True))
            prob = exponent / jnp.sum(exponent, axis=-1, keepdims=True)
            prob_ref[2 * pair + half] = prob
            outs.append(dot(prob.astype(BF16), values, NN))
        attn_ref[pair] = jnp.where(lane < HEAD_DIM, outs[0], outs[1]).astype(BF16)


def backward_body(
    own_sum_ref,
    far_sum_ref,
    mate_sum_ref,
    dec_ref,
    out_weight_ref,
    query_ref,
    key_ref,
    value_ref,
    far_ref,
    mate_ref,
    prob_ref,
    after_ref,
    states_ref,
    grad_query_ref,
    to_far_ref,
    own_ref,
    to_mate_ref,
    dec_s,
):
    dec_s[...] = jnp.zeros(dec_s.shape, BF16)
    dec_s[0:VARS, :] = dec_ref.ready()[...]
    dec = dec_s[...]
    total = own_sum_ref.ready()[...] + far_sum_ref.ready()[...] + mate_sum_ref.ready()[...]
    grad_states = dot(
        jnp.concatenate(split(total), axis=1), jnp.concatenate([dec, dec], axis=0), NN
    ).astype(BF16)
    states_ref[0] = grad_states
    grad_out = dot(grad_states, out_weight_ref.ready()[...], NT).astype(BF16)
    query_ref, key_ref, value_ref = query_ref.ready(), key_ref.ready(), value_ref.ready()
    far_ref, mate_ref, prob_ref = far_ref.ready(), mate_ref.ready(), prob_ref.ready()
    masks = pair_masks(BF16)
    lane = lax.broadcasted_iota(jnp.int32, (1, PAIR), 1)
    first = lane < HEAD_DIM
    for pair in range(HEADS // 2):
        cols = slice(pair * PAIR, (pair + 1) * PAIR)
        vcols = slice(ATT + pair * PAIR, ATT + (pair + 1) * PAIR)
        query = query_ref[0, :, cols]
        keys = band_blocks(far_ref, key_ref, mate_ref, pair, 0)
        values = band_blocks(far_ref, value_ref, mate_ref, pair, ATT)
        grads = grad_out[:, cols]
        key_terms, value_terms, query_terms = [], [], []
        for half in range(2):
            prob = prob_ref[2 * pair + half]
            grad_prob = dot(grads * masks[half], values, NT)
            delta = jnp.sum(prob * grad_prob, axis=-1, keepdims=True)
            grad_scores = (prob * (grad_prob - delta)).astype(BF16)
            value_terms.append(dot(prob.astype(BF16), grads, TN))
            query_terms.append(dot(grad_scores, keys, NN))
            key_terms.append(dot(grad_scores, query, TN))
        grad_query_ref[0, :, cols] = (
            jnp.where(first, query_terms[0], query_terms[1]) * SCALE
        ).astype(BF16)
        key_term = jnp.where(first, key_terms[0], key_terms[1]) * SCALE
        value_term = jnp.where(first, value_terms[0], value_terms[1])
        for term, where in ((key_term, cols), (value_term, vcols)):
            to_far_ref[:, where] = term[0:NODES].astype(BF16)
            own_ref[:, where] = term[NODES : 2 * NODES]
            to_mate_ref[:, where] = term[2 * NODES : SPAN].astype(BF16)


def join_body(own_ref, far_ref, mate_ref, key_ref, value_ref, done_ref):
    done_ref[...] = jnp.zeros(done_ref.shape, F32)
    own_ref, far_ref, mate_ref = own_ref.ready(), far_ref.ready(), mate_ref.ready()
    for first, ref in ((0, key_ref), (ATT, value_ref)):
        cols = slice(first, first + ATT)
        ref[0] = (
            own_ref[:, cols] + far_ref[:, cols].astype(F32) + mate_ref[:, cols].astype(F32)
        ).astype(BF16)


def swap_far(x):
    pairs = [(i, i + 1) for i in range(1, 63, 2)]
    return lax.ppermute(x, SPACE, pairs + [(target, source) for source, target in pairs])


def swap_mate(x):
    return lax.ppermute(x, "c", [(0, 1), (1, 0)])


def exchange(x, axes):
    return lax.all_to_all(x, axes, split_axis=0, concat_axis=0, tiled=True)


def per_device(
    node_states,
    query,
    key,
    value,
    out_weight,
    dec_weight,
    target,
    area_weight,
    var_weight,
    edges,
    edge_weight,
    windows,
):
    band = lax.axis_index(SPACE).astype(jnp.int32).reshape(1)
    member = (2 * lax.axis_index("y")).astype(jnp.int32).reshape(1)
    proj = call(
        project_body,
        shape((VARS_SUB, NODES), BF16),
        "ll",
        (node_states, dec_weight),
        scratch=[pltpu.VMEM((VARS_SUB, WIDTH), BF16)],
        limit=WHOLE,
    )
    other = lax.ppermute(proj, "zh", [(0, 1), (1, 0)])
    packed = call(
        pack_body,
        shape((NODES, 2 * WIDTH), BF16),
        "aaaa",
        (node_states, key, value, proj),
        scratch=[pltpu.SemaphoreType.DMA((3,))],
        limit=WHOLE,
    )
    mate_band, far_band = swap_mate(packed), swap_far(packed)
    pairs = call(
        pair_body,
        shape((4, 2 * VARS_SUB, NODES), BF16),
        "ll",
        (proj, other),
        cost=LONG,
    )
    mid = exchange(pairs, "y")
    prob, attn = call(
        forward_body,
        (shape((HEADS, NODES, SPAN), F32), shape((ATT // PAIR, NODES, PAIR), BF16)),
        "sslllkk",
        (band, windows, query, key, value, mate_band, far_band),
    )
    mix, weight = call(
        weights_body,
        (shape((SPAN, POINTS), BF16), shape((VARS_SUB, POINTS), F32)),
        "svvvv",
        (band, edges, edge_weight, area_weight.reshape(1, -1), var_weight.reshape(1, -1)),
    )
    halo = jnp.concatenate([mid.reshape(-1, NODES), attn.reshape(-1, PAIR)], axis=0)
    mate_halo, far_halo = swap_mate(halo), swap_far(halo)
    block = shape((NODES, VARS_LANE), F32)
    terms, to_far, own, to_mate = call(
        crps_body,
        (shape((NEAR_SIZE, ROWS, VARS_LANE), BF16), block, block, block),
        "svvvvvvlltt",
        (
            member,
            mate_halo,
            mid,
            far_halo,
            mix,
            weight,
            target,
            attn,
            node_states,
            mate_band,
            far_band,
        ),
        scratch=[
            pltpu.VMEM((MEMBERS, VARS_SUB, POINTS), F32),
            pltpu.VMEM((VARS_LANE, POINTS), BF16),
        ],
    )
    near = exchange(terms, NEAR)
    mate_sum, far_sum = swap_mate(to_mate), swap_far(to_far)
    near_sums = call(
        near_body, shape((FAR_SIZE, ROWS, VARS_LANE), BF16), "v", (near,), cost=LONG
    )
    along = exchange(near_sums, FAR)
    wide = (NODES, 2 * ATT)
    flag = shape((8, 128), F32)
    grad_states, grad_query, kv_far, kv_own, kv_mate = call(
        backward_body,
        (
            shape((1, NODES, WIDTH), BF16),
            shape((1, NODES, ATT), BF16),
            shape(wide, BF16),
            shape(wide, F32),
            shape(wide, BF16),
        ),
        "llllllllkkla",
        (
            own,
            far_sum,
            mate_sum,
            dec_weight,
            out_weight,
            query,
            key,
            value,
            far_band,
            mate_band,
            prob,
            near_sums,
        ),
        scratch=[pltpu.VMEM((VARS_LANE, WIDTH), BF16)],
        limit=WHOLE,
        cost=LONG,
    )
    far_sums = call(
        sum_body,
        shape((NEAR_SIZE, ROWS, VARS_LANE), BF16),
        "v",
        (along,),
        cost=LONG,
    )
    everything = exchange(far_sums, NEAR)
    mate_term, far_term = swap_mate(kv_mate), swap_far(kv_far)
    grad_key, grad_value, joined = call(
        join_body,
        (shape((1, NODES, ATT), BF16), shape((1, NODES, ATT), BF16), flag),
        "lll",
        (kv_own, far_term, mate_term),
        cost=LONG,
    )
    grad_wo, grad_dec = call(
        final_body,
        (shape((8, WIDTH), F32), shape((VARS, WIDTH), F32)),
        "svva",
        (band, everything, dec_weight, joined),
        scratch=[pltpu.VMEM((VARS_LANE, WIDTH), BF16), pltpu.VMEM((WO_ROWS, WIDTH), F32)],
    )
    return grad_states, grad_query, grad_key, grad_value, grad_wo, grad_dec


def solution(mesh):
    fine = Mesh(mesh.devices.reshape(SIZES), AXES)
    in_specs = (
        P(ENS, SPACE, None),
        P(ENS, SPACE, None),
        P(ENS, SPACE, None),
        P(ENS, SPACE, None),
        P(),
        P(),
        P(None, SPACE),
        P(SPACE),
        P(),
        P(None, SPACE),
        P(None, SPACE),
        P(None, SPACE),
    )
    out_specs = (
        P(ENS, SPACE, None),
        P(ENS, SPACE, None),
        P(ENS, SPACE, None),
        P(ENS, SPACE, None),
        P(SPACE, None),
        P(),
    )
    return jax.shard_map(
        per_device, mesh=fine, in_specs=in_specs, out_specs=out_specs, check_vma=False
    )
```

```python
import math

import jax
import jax.numpy as jnp
from jax import lax
from jax.experimental import pallas as pl
from jax.experimental.pallas import tpu as pltpu
from jax.sharding import Mesh
from jax.sharding import PartitionSpec as P

HEADS = 8
HEAD_DIM = 64
PAIR = 2 * HEAD_DIM
VARS = 100
VARS_SUB = 112
VARS_LANE = 128
MEMBERS = 8
NODES = 128
POINTS = 1024
SPAN = 3 * NODES
WIDTH = 1024
ATT = 512
SMOOTH_SQUARE = 0.0625
MASKED_SCORE = -1e30
SCALE = 1.0 / math.sqrt(HEAD_DIM)

AXES = ("zh", "y", "x", "zl", "c")
SIZES = (2, 4, 4, 8, 2)
ENS = ("zh", "y")
SPACE = ("x", "zl", "c")
NEAR = ("y", "x", "c")
NEAR_SIZE = 32
FAR = ("zh", "zl")
FAR_SIZE = 16
DEC_ROWS = WIDTH // NEAR_SIZE
WO_ROWS = ATT // NEAR_SIZE
ROWS = DEC_ROWS + WO_ROWS
OWN_ROWS = 2
SENT = DEC_ROWS + 8

WHOLE = 58 * 2**20
LONG = 2 * 10**10

F32 = jnp.float32
BF16 = jnp.bfloat16
NN = (((1,), (0,)), ((), ()))
NT = (((1,), (1,)), ((), ()))
TN = (((0,), (0,)), ((), ()))


def dot(a, b, dims):
    return lax.dot_general(a, b, dims, preferred_element_type=F32)


class Landing:
    def __init__(self, source, target, sem):
        self.target = target
        self.copy = pltpu.make_async_copy(source, target, sem)
        self.copy.start()

    def ready(self):
        self.copy.wait()
        return self.target


def call(body, out_shape, spaces, args, scratch=(), cost=10**8, limit=24 * 2**20):
    kinds = {
        "s": pl.BlockSpec(memory_space=pltpu.SMEM),
        "v": pl.BlockSpec(memory_space=pltpu.VMEM),
    }
    left = pl.BlockSpec(memory_space=pl.ANY)
    specs = [kinds.get(space, left) for space in spaces]
    landed = [i for i, space in enumerate(spaces) if space in "ltk"]
    outs = len(out_shape) if isinstance(out_shape, tuple) else 1
    if landed:
        targets = [
            pltpu.VMEM(args[i].shape if spaces[i] == "l" else (NODES, WIDTH), args[i].dtype)
            for i in landed
        ]
        scratch = [*targets, pltpu.SemaphoreType.DMA((len(landed),)), *scratch]

    def kernel(*refs):
        inputs = list(refs[: len(args)])
        results = refs[len(args) : len(args) + outs]
        rest = refs[len(args) + outs :]
        if landed:
            count = len(landed)
            for k, i in enumerate(landed):
                source = inputs[i]
                if spaces[i] == "t":
                    source = source.at[:, pl.ds(0, WIDTH)]
                if spaces[i] == "k":
                    source = source.at[:, pl.ds(WIDTH, WIDTH)]
                inputs[i] = Landing(source, rest[k], rest[count].at[k])
            rest = rest[count + 1 :]
        body(*inputs, *results, *rest)

    return pl.pallas_call(
        kernel,
        out_shape=out_shape,
        in_specs=specs,
        scratch_shapes=list(scratch),
        compiler_params=pltpu.CompilerParams(vmem_limit_bytes=limit),
        cost_estimate=pl.CostEstimate(flops=cost, bytes_accessed=10**6, transcendentals=0),
    )(*args)


def shape(dims, dtype):
    return jax.ShapeDtypeStruct(dims, dtype)


def smooth_slope(t):
    return t * lax.rsqrt(t * t + SMOOTH_SQUARE)


def split(x):
    high = x.astype(BF16)
    return high, (x - high.astype(F32)).astype(BF16)


def project_body(states_ref, dec_ref, proj_ref, pad_s):
    pad_s[...] = jnp.zeros(pad_s.shape, BF16)
    pad_s[0:VARS, :] = dec_ref.ready()[...]
    proj_ref[...] = dot(pad_s[...], states_ref.ready()[0], NT).astype(BF16)


def pack_body(states_hbm, key_hbm, value_hbm, after_ref, out_ref, sems):
    copies = [
        pltpu.make_async_copy(states_hbm.at[0], out_ref.at[:, pl.ds(0, WIDTH)], sems.at[0]),
        pltpu.make_async_copy(key_hbm.at[0], out_ref.at[:, pl.ds(WIDTH, ATT)], sems.at[1]),
        pltpu.make_async_copy(value_hbm.at[0], out_ref.at[:, pl.ds(WIDTH + ATT, ATT)], sems.at[2]),
    ]
    for copy in copies:
        copy.start()
    for copy in copies:
        copy.wait()


def pair_body(own_ref, other_ref, out_ref):
    own_ref, other_ref = own_ref.ready(), other_ref.ready()
    for i in range(out_ref.shape[0]):
        out_ref[i, 0:VARS_SUB, :] = own_ref[...]
        out_ref[i, VARS_SUB : 2 * VARS_SUB, :] = other_ref[...]


def bases(band):
    side = 2 * lax.rem(band, 2) - 1
    return (band + side) * NODES, band * NODES, (band - side) * NODES


def weights_body(band_ref, edges_ref, edge_weight_ref, area_ref, var_ref, mix_ref, weight_ref):
    edges = edges_ref[...]
    for part, base in enumerate(bases(band_ref[0])):
        place = lax.broadcasted_iota(jnp.int32, (NODES, POINTS), 0) + base
        mix = jnp.zeros((NODES, POINTS), F32)
        for slot in range(3):
            mix = mix + jnp.where(
                edges[slot : slot + 1, :] == place, edge_weight_ref[slot : slot + 1, :], 0.0
            )
        mix_ref[part * NODES : (part + 1) * NODES, :] = mix.astype(BF16)
    row = jnp.concatenate([var_ref[...], jnp.zeros((1, VARS_LANE - VARS), F32)], axis=1)
    column = jnp.transpose(jnp.broadcast_to(row, (VARS_LANE, VARS_LANE)))[0:VARS_SUB, 0:1]
    weight_ref[...] = column * area_ref[...]


def crps_body(
    member_ref,
    mate_ref,
    mid_ref,
    far_ref,
    mix_ref,
    weight_ref,
    target_ref,
    attn_ref,
    states_ref,
    mate_states_ref,
    far_states_ref,
    after_ref,
    terms_ref,
    to_far_ref,
    own_ref,
    to_mate_ref,
    pred_s,
    grad_s,
):
    mix = mix_ref[...]
    for member in range(MEMBERS):
        rows = slice(member * VARS_SUB, (member + 1) * VARS_SUB)
        half = slice((member % 2) * VARS_SUB, (member % 2 + 1) * VARS_SUB)
        proj = jnp.concatenate([far_ref[rows], mid_ref[member // 2, half], mate_ref[rows]], axis=1)
        pred_s[member] = dot(proj, mix, NN)
    grad_s[...] = jnp.zeros(grad_s.shape, BF16)
    me = member_ref[0]
    for first in range(0, VARS, 16):
        rows = min(16, VARS - first)
        mine = pred_s[me, first : first + rows, :]
        total = jnp.zeros_like(mine)
        for member in range(MEMBERS):
            total = total + smooth_slope(mine - pred_s[member, first : first + rows, :])
        slopes = smooth_slope(mine - target_ref[first : first + rows, :]) - total * (
            1.0 / (MEMBERS - 1)
        )
        grad_s[first : first + rows, :] = (weight_ref[first : first + rows, :] * slopes).astype(
            BF16
        )
    grads = grad_s[...]
    sums = dot(mix, grads, NT)
    to_far_ref[...] = sums[0:NODES]
    own_ref[...] = sums[NODES : 2 * NODES]
    to_mate_ref[...] = sums[2 * NODES : SPAN]
    turned = dot(grads, mix, NT).astype(BF16)
    bands = (far_states_ref.ready(), states_ref.ready().at[0], mate_states_ref.ready())
    for block in range(WIDTH // NODES):
        cols = slice(block * NODES, (block + 1) * NODES)
        states = jnp.concatenate([band[:, cols] for band in bands], axis=0)
        dec = jnp.transpose(dot(turned, states, NN)).astype(BF16)
        count = NODES // DEC_ROWS
        terms_ref[block * count : (block + 1) * count, 0:DEC_ROWS, :] = dec.reshape(
            count, DEC_ROWS, VARS_LANE
        )
    attn_ref = attn_ref.ready()
    source = lax.broadcasted_iota(jnp.int32, (PAIR, PAIR), 1)
    place = ((source & 6) << 4) + ((source & 8) << 1) + ((source & 112) >> 3) + (source & 1)
    order = (lax.broadcasted_iota(jnp.int32, (PAIR, PAIR), 0) == place).astype(BF16)
    for block in range(ATT // PAIR):
        first = MEMBERS * VARS_SUB + block * NODES
        rows = slice(first, first + NODES)
        attn = jnp.concatenate([far_ref[rows], attn_ref[block], mate_ref[rows]], axis=0)
        wo = dot(order, dot(turned, attn, NN).astype(BF16), NT).astype(BF16)
        for part in range(NODES // WO_ROWS):
            row, core = part // 2, part % 2
            terms_ref[(row * 4 + block) * 2 + core, DEC_ROWS:ROWS, :] = wo[
                part * WO_ROWS : (part + 1) * WO_ROWS
            ]


def total_of(in_ref):
    total = in_ref[0].astype(F32)
    for i in range(1, in_ref.shape[0]):
        total = total + in_ref[i].astype(F32)
    return total


def near_body(in_ref, out_ref):
    total = total_of(in_ref)
    dec = total[0:DEC_ROWS].astype(BF16)
    rest = jnp.zeros((SENT - DEC_ROWS - OWN_ROWS, VARS_LANE), F32)
    for i in range(FAR_SIZE):
        first = DEC_ROWS + OWN_ROWS * (i % 8)
        wo = jnp.concatenate([total[first : first + OWN_ROWS], rest], axis=0)
        out_ref[i, 0:DEC_ROWS, :] = dec
        out_ref[i, DEC_ROWS:SENT, :] = wo.astype(BF16)


def sum_body(in_ref, out_ref):
    total = total_of(in_ref).astype(BF16)
    for i in range(NEAR_SIZE):
        out_ref[i] = total


def final_body(band_ref, all_ref, dec_ref, after_ref, wo_ref, grad_dec_ref, dec_s):
    dec_s[...] = jnp.zeros(dec_s.shape, BF16)
    dec_s[0:VARS, :] = dec_ref[...]
    column, core = lax.div(band_ref[0], 16), lax.rem(band_ref[0], 2)
    rows = [
        all_ref[(row * 4 + column) * 2 + core, DEC_ROWS:SENT, :].astype(F32)[0:OWN_ROWS]
        for row in range(4)
    ]
    wo_ref[...] = dot(jnp.concatenate(rows, axis=0).astype(BF16), dec_s[...], NN)
    dec = all_ref[:, 0:DEC_ROWS, :].astype(F32).reshape(WIDTH, VARS_LANE)
    grad_dec_ref[...] = jnp.transpose(dec)[0:VARS, :]


def pair_masks(dtype):
    lane = lax.broadcasted_iota(jnp.int32, (1, PAIR), 1)
    return (lane < HEAD_DIM).astype(dtype), (lane >= HEAD_DIM).astype(dtype)


def band_blocks(far_ref, own_ref, mate_ref, pair, first):
    cols = slice(pair * PAIR, (pair + 1) * PAIR)
    side = slice(first + pair * PAIR, first + (pair + 1) * PAIR)
    return jnp.concatenate([far_ref[:, side], own_ref[0, :, cols], mate_ref[:, side]], axis=0)


def probabilities(inside, query_ref, key_ref, mate_ref, far_ref, pair):
    masks = pair_masks(BF16)
    query = query_ref[0, :, pair * PAIR : (pair + 1) * PAIR]
    keys = band_blocks(far_ref, key_ref, mate_ref, pair, 0)
    probs = []
    for half in range(2):
        scores = dot(query * masks[half], keys, NT) * SCALE
        scores = jnp.where(inside, scores, MASKED_SCORE)
        exponent = jnp.exp(scores - jnp.max(scores, axis=-1, keepdims=True))
        probs.append(exponent / jnp.sum(exponent, axis=-1, keepdims=True))
    return probs


def window(band_ref, windows_ref):
    lanes = lax.broadcasted_iota(jnp.int32, (1, NODES), 1)
    place = jnp.concatenate([lanes + base for base in bases(band_ref[0])], axis=1)
    return (place >= windows_ref[0, 0]) & (place < windows_ref[1, 0])


def forward_body(
    band_ref, windows_ref, query_ref, key_ref, value_ref, mate_ref, far_ref, attn_ref
):
    query_ref, key_ref, value_ref = query_ref.ready(), key_ref.ready(), value_ref.ready()
    far_ref, mate_ref = far_ref.ready(), mate_ref.ready()
    inside = window(band_ref, windows_ref)
    lane = lax.broadcasted_iota(jnp.int32, (1, PAIR), 1)
    for pair in range(HEADS // 2):
        values = band_blocks(far_ref, value_ref, mate_ref, pair, ATT)
        outs = [
            dot(prob.astype(BF16), values, NN)
            for prob in probabilities(inside, query_ref, key_ref, mate_ref, far_ref, pair)
        ]
        attn_ref[pair] = jnp.where(lane < HEAD_DIM, outs[0], outs[1]).astype(BF16)


def prob_body(
    band_ref, windows_ref, query_ref, key_ref, mate_ref, far_ref, after_ref, prob_ref, done_ref
):
    done_ref[...] = jnp.zeros(done_ref.shape, F32)
    query_ref, key_ref = query_ref.ready(), key_ref.ready()
    far_ref, mate_ref = far_ref.ready(), mate_ref.ready()
    inside = window(band_ref, windows_ref)
    for pair in range(HEADS // 2):
        probs = probabilities(inside, query_ref, key_ref, mate_ref, far_ref, pair)
        prob_ref[2 * pair] = probs[0]
        prob_ref[2 * pair + 1] = probs[1]


def backward_body(
    own_sum_ref,
    far_sum_ref,
    mate_sum_ref,
    dec_ref,
    out_weight_ref,
    query_ref,
    key_ref,
    value_ref,
    far_ref,
    mate_ref,
    prob_ref,
    after_ref,
    states_ref,
    grad_query_ref,
    to_far_ref,
    own_ref,
    to_mate_ref,
    dec_s,
):
    dec_s[...] = jnp.zeros(dec_s.shape, BF16)
    dec_s[0:VARS, :] = dec_ref.ready()[...]
    dec = dec_s[...]
    total = own_sum_ref.ready()[...] + far_sum_ref.ready()[...] + mate_sum_ref.ready()[...]
    grad_states = dot(
        jnp.concatenate(split(total), axis=1), jnp.concatenate([dec, dec], axis=0), NN
    ).astype(BF16)
    states_ref[0] = grad_states
    grad_out = dot(grad_states, out_weight_ref.ready()[...], NT).astype(BF16)
    query_ref, key_ref, value_ref = query_ref.ready(), key_ref.ready(), value_ref.ready()
    far_ref, mate_ref, prob_ref = far_ref.ready(), mate_ref.ready(), prob_ref.ready()
    masks = pair_masks(BF16)
    lane = lax.broadcasted_iota(jnp.int32, (1, PAIR), 1)
    first = lane < HEAD_DIM
    for pair in range(HEADS // 2):
        cols = slice(pair * PAIR, (pair + 1) * PAIR)
        vcols = slice(ATT + pair * PAIR, ATT + (pair + 1) * PAIR)
        query = query_ref[0, :, cols]
        keys = band_blocks(far_ref, key_ref, mate_ref, pair, 0)
        values = band_blocks(far_ref, value_ref, mate_ref, pair, ATT)
        grads = grad_out[:, cols]
        key_terms, value_terms, query_terms = [], [], []
        for half in range(2):
            prob = prob_ref[2 * pair + half]
            grad_prob = dot(grads * masks[half], values, NT)
            delta = jnp.sum(prob * grad_prob, axis=-1, keepdims=True)
            grad_scores = (prob * (grad_prob - delta)).astype(BF16)
            value_terms.append(dot(prob.astype(BF16), grads, TN))
            query_terms.append(dot(grad_scores, keys, NN))
            key_terms.append(dot(grad_scores, query, TN))
        grad_query_ref[0, :, cols] = (
            jnp.where(first, query_terms[0], query_terms[1]) * SCALE
        ).astype(BF16)
        key_term = jnp.where(first, key_terms[0], key_terms[1]) * SCALE
        value_term = jnp.where(first, value_terms[0], value_terms[1])
        for term, where in ((key_term, cols), (value_term, vcols)):
            to_far_ref[:, where] = term[0:NODES].astype(BF16)
            own_ref[:, where] = term[NODES : 2 * NODES]
            to_mate_ref[:, where] = term[2 * NODES : SPAN].astype(BF16)


def join_body(own_ref, far_ref, mate_ref, key_ref, value_ref, done_ref):
    done_ref[...] = jnp.zeros(done_ref.shape, F32)
    own_ref, far_ref, mate_ref = own_ref.ready(), far_ref.ready(), mate_ref.ready()
    for first, ref in ((0, key_ref), (ATT, value_ref)):
        cols = slice(first, first + ATT)
        ref[0] = (
            own_ref[:, cols] + far_ref[:, cols].astype(F32) + mate_ref[:, cols].astype(F32)
        ).astype(BF16)


def swap_far(x):
    pairs = [(i, i + 1) for i in range(1, 63, 2)]
    return lax.ppermute(x, SPACE, pairs + [(target, source) for source, target in pairs])


def swap_mate(x):
    return lax.ppermute(x, "c", [(0, 1), (1, 0)])


def exchange(x, axes):
    return lax.all_to_all(x, axes, split_axis=0, concat_axis=0, tiled=True)


def per_device(
    node_states,
    query,
    key,
    value,
    out_weight,
    dec_weight,
    target,
    area_weight,
    var_weight,
    edges,
    edge_weight,
    windows,
):
    band = lax.axis_index(SPACE).astype(jnp.int32).reshape(1)
    member = (2 * lax.axis_index("y")).astype(jnp.int32).reshape(1)
    proj = call(
        project_body,
        shape((VARS_SUB, NODES), BF16),
        "ll",
        (node_states, dec_weight),
        scratch=[pltpu.VMEM((VARS_SUB, WIDTH), BF16)],
        limit=WHOLE,
    )
    other = lax.ppermute(proj, "zh", [(0, 1), (1, 0)])
    packed = call(
        pack_body,
        shape((NODES, 2 * WIDTH), BF16),
        "aaaa",
        (node_states, key, value, proj),
        scratch=[pltpu.SemaphoreType.DMA((3,))],
        limit=WHOLE,
    )
    mate_band, far_band = swap_mate(packed), swap_far(packed)
    pairs = call(
        pair_body,
        shape((4, 2 * VARS_SUB, NODES), BF16),
        "ll",
        (proj, other),
        cost=LONG,
    )
    mid = exchange(pairs, "y")
    attn = call(
        forward_body,
        shape((ATT // PAIR, NODES, PAIR), BF16),
        "sslllkk",
        (band, windows, query, key, value, mate_band, far_band),
    )
    mix, weight = call(
        weights_body,
        (shape((SPAN, POINTS), BF16), shape((VARS_SUB, POINTS), F32)),
        "svvvv",
        (band, edges, edge_weight, area_weight.reshape(1, -1), var_weight.reshape(1, -1)),
    )
    halo = jnp.concatenate([mid.reshape(-1, NODES), attn.reshape(-1, PAIR)], axis=0)
    mate_halo, far_halo = swap_mate(halo), swap_far(halo)
    flag = shape((8, 128), F32)
    prob, done = call(
        prob_body,
        (shape((HEADS, NODES, SPAN), F32), flag),
        "ssllkka",
        (band, windows, query, key, mate_band, far_band, halo),
        cost=LONG,
    )
    block = shape((NODES, VARS_LANE), F32)
    terms, to_far, own, to_mate = call(
        crps_body,
        (shape((NEAR_SIZE, ROWS, VARS_LANE), BF16), block, block, block),
        "svvvvvvllttv",
        (
            member,
            mate_halo,
            mid,
            far_halo,
            mix,
            weight,
            target,
            attn,
            node_states,
            mate_band,
            far_band,
            done,
        ),
        scratch=[
            pltpu.VMEM((MEMBERS, VARS_SUB, POINTS), F32),
            pltpu.VMEM((VARS_LANE, POINTS), BF16),
        ],
    )
    near = exchange(terms, NEAR)
    mate_sum, far_sum = swap_mate(to_mate), swap_far(to_far)
    near_sums = call(
        near_body, shape((FAR_SIZE, SENT, VARS_LANE), BF16), "v", (near,), cost=LONG
    )
    along = exchange(near_sums, FAR)
    wide = (NODES, 2 * ATT)
    grad_states, grad_query, kv_far, kv_own, kv_mate = call(
        backward_body,
        (
            shape((1, NODES, WIDTH), BF16),
            shape((1, NODES, ATT), BF16),
            shape(wide, BF16),
            shape(wide, F32),
            shape(wide, BF16),
        ),
        "llllllllkkla",
        (
            own,
            far_sum,
            mate_sum,
            dec_weight,
            out_weight,
            query,
            key,
            value,
            far_band,
            mate_band,
            prob,
            near_sums,
        ),
        scratch=[pltpu.VMEM((VARS_LANE, WIDTH), BF16)],
        limit=WHOLE,
        cost=LONG,
    )
    far_sums = call(
        sum_body,
        shape((NEAR_SIZE, SENT, VARS_LANE), BF16),
        "v",
        (along,),
        cost=LONG,
    )
    everything = exchange(far_sums, NEAR)
    mate_term, far_term = swap_mate(kv_mate), swap_far(kv_far)
    grad_key, grad_value, joined = call(
        join_body,
        (shape((1, NODES, ATT), BF16), shape((1, NODES, ATT), BF16), flag),
        "lll",
        (kv_own, far_term, mate_term),
        cost=LONG,
    )
    grad_wo, grad_dec = call(
        final_body,
        (shape((8, WIDTH), F32), shape((VARS, WIDTH), F32)),
        "svva",
        (band, everything, dec_weight, joined),
        scratch=[pltpu.VMEM((VARS_LANE, WIDTH), BF16)],
    )
    return grad_states, grad_query, grad_key, grad_value, grad_wo, grad_dec


def solution(mesh):
    fine = Mesh(mesh.devices.reshape(SIZES), AXES)
    in_specs = (
        P(ENS, SPACE, None),
        P(ENS, SPACE, None),
        P(ENS, SPACE, None),
        P(ENS, SPACE, None),
        P(),
        P(),
        P(None, SPACE),
        P(SPACE),
        P(),
        P(None, SPACE),
        P(None, SPACE),
        P(None, SPACE),
    )
    out_specs = (
        P(ENS, SPACE, None),
        P(ENS, SPACE, None),
        P(ENS, SPACE, None),
        P(ENS, SPACE, None),
        P(SPACE, None),
        P(),
    )
    return jax.shard_map(
        per_device, mesh=fine, in_specs=in_specs, out_specs=out_specs, check_vma=False
    )
```

```python
import math

import jax
import jax.numpy as jnp
from jax import lax
from jax.experimental import pallas as pl
from jax.experimental.pallas import tpu as pltpu
from jax.sharding import Mesh
from jax.sharding import PartitionSpec as P

HEADS = 8
HEAD_DIM = 64
PAIR = 2 * HEAD_DIM
VARS = 100
VARS_SUB = 112
VARS_LANE = 128
MEMBERS = 8
NODES = 128
POINTS = 1024
SPAN = 3 * NODES
WIDTH = 1024
ATT = 512
SMOOTH_SQUARE = 0.0625
MASKED_SCORE = -1e30
SCALE = 1.0 / math.sqrt(HEAD_DIM)

AXES = ("zh", "y", "x", "zl", "c")
SIZES = (2, 4, 4, 8, 2)
ENS = ("zh", "y")
SPACE = ("x", "zl", "c")
NEAR = ("y", "x", "c")
NEAR_SIZE = 32
FAR = ("zh", "zl")
FAR_SIZE = 16
DEC_ROWS = WIDTH // NEAR_SIZE
WO_ROWS = ATT // NEAR_SIZE
ROWS = DEC_ROWS + WO_ROWS
OWN_ROWS = 2
SENT = DEC_ROWS + 8

WHOLE = 58 * 2**20
LONG = 2 * 10**10

F32 = jnp.float32
BF16 = jnp.bfloat16
NN = (((1,), (0,)), ((), ()))
NT = (((1,), (1,)), ((), ()))
TN = (((0,), (0,)), ((), ()))


def dot(a, b, dims):
    return lax.dot_general(a, b, dims, preferred_element_type=F32)


class Landing:
    def __init__(self, source, target, sem):
        self.target = target
        self.copy = pltpu.make_async_copy(source, target, sem)
        self.copy.start()

    def ready(self):
        self.copy.wait()
        return self.target


def call(body, out_shape, spaces, args, scratch=(), cost=10**8, limit=24 * 2**20):
    kinds = {
        "s": pl.BlockSpec(memory_space=pltpu.SMEM),
        "v": pl.BlockSpec(memory_space=pltpu.VMEM),
    }
    left = pl.BlockSpec(memory_space=pl.ANY)
    specs = [kinds.get(space, left) for space in spaces]
    landed = [i for i, space in enumerate(spaces) if space in "ltk"]
    outs = len(out_shape) if isinstance(out_shape, tuple) else 1
    if landed:
        targets = [
            pltpu.VMEM(args[i].shape if spaces[i] == "l" else (NODES, WIDTH), args[i].dtype)
            for i in landed
        ]
        scratch = [*targets, pltpu.SemaphoreType.DMA((len(landed),)), *scratch]

    def kernel(*refs):
        inputs = list(refs[: len(args)])
        results = refs[len(args) : len(args) + outs]
        rest = refs[len(args) + outs :]
        if landed:
            count = len(landed)
            for k, i in enumerate(landed):
                source = inputs[i]
                if spaces[i] == "t":
                    source = source.at[:, pl.ds(0, WIDTH)]
                if spaces[i] == "k":
                    source = source.at[:, pl.ds(WIDTH, WIDTH)]
                inputs[i] = Landing(source, rest[k], rest[count].at[k])
            rest = rest[count + 1 :]
        body(*inputs, *results, *rest)

    return pl.pallas_call(
        kernel,
        out_shape=out_shape,
        in_specs=specs,
        scratch_shapes=list(scratch),
        compiler_params=pltpu.CompilerParams(vmem_limit_bytes=limit),
        cost_estimate=pl.CostEstimate(flops=cost, bytes_accessed=10**6, transcendentals=0),
    )(*args)


def shape(dims, dtype):
    return jax.ShapeDtypeStruct(dims, dtype)


def smooth_slope(t):
    return t * lax.rsqrt(t * t + SMOOTH_SQUARE)


def split(x):
    high = x.astype(BF16)
    return high, (x - high.astype(F32)).astype(BF16)


def project_body(states_ref, dec_ref, proj_ref, pad_s):
    pad_s[...] = jnp.zeros(pad_s.shape, BF16)
    pad_s[0:VARS, :] = dec_ref.ready()[...]
    proj_ref[...] = dot(pad_s[...], states_ref.ready()[0], NT).astype(BF16)


def pack_body(states_hbm, key_hbm, value_hbm, after_ref, out_ref, sems):
    copies = [
        pltpu.make_async_copy(states_hbm.at[0], out_ref.at[:, pl.ds(0, WIDTH)], sems.at[0]),
        pltpu.make_async_copy(key_hbm.at[0], out_ref.at[:, pl.ds(WIDTH, ATT)], sems.at[1]),
        pltpu.make_async_copy(value_hbm.at[0], out_ref.at[:, pl.ds(WIDTH + ATT, ATT)], sems.at[2]),
    ]
    for copy in copies:
        copy.start()
    for copy in copies:
        copy.wait()


def pair_body(own_ref, other_ref, out_ref):
    own_ref, other_ref = own_ref.ready(), other_ref.ready()
    for i in range(out_ref.shape[0]):
        out_ref[i, 0:VARS_SUB, :] = own_ref[...]
        out_ref[i, VARS_SUB : 2 * VARS_SUB, :] = other_ref[...]


def bases(band):
    side = 2 * lax.rem(band, 2) - 1
    return (band + side) * NODES, band * NODES, (band - side) * NODES


def weights_body(band_ref, edges_ref, edge_weight_ref, area_ref, var_ref, mix_ref, weight_ref):
    edges = edges_ref[...]
    for part, base in enumerate(bases(band_ref[0])):
        place = lax.broadcasted_iota(jnp.int32, (NODES, POINTS), 0) + base
        mix = jnp.zeros((NODES, POINTS), F32)
        for slot in range(3):
            mix = mix + jnp.where(
                edges[slot : slot + 1, :] == place, edge_weight_ref[slot : slot + 1, :], 0.0
            )
        mix_ref[part * NODES : (part + 1) * NODES, :] = mix.astype(BF16)
    row = jnp.concatenate([var_ref[...], jnp.zeros((1, VARS_LANE - VARS), F32)], axis=1)
    column = jnp.transpose(jnp.broadcast_to(row, (VARS_LANE, VARS_LANE)))[0:VARS_SUB, 0:1]
    weight_ref[...] = column * area_ref[...]


def crps_body(
    member_ref,
    mate_ref,
    mid_ref,
    far_ref,
    mix_ref,
    weight_ref,
    target_ref,
    attn_ref,
    states_ref,
    mate_states_ref,
    far_states_ref,
    after_ref,
    terms_ref,
    to_far_ref,
    own_ref,
    to_mate_ref,
    pred_s,
    grad_s,
):
    mix = mix_ref[...]
    for member in range(MEMBERS):
        rows = slice(member * VARS_SUB, (member + 1) * VARS_SUB)
        half = slice((member % 2) * VARS_SUB, (member % 2 + 1) * VARS_SUB)
        proj = jnp.concatenate([far_ref[rows], mid_ref[member // 2, half], mate_ref[rows]], axis=1)
        pred_s[member] = dot(proj, mix, NN)
    grad_s[...] = jnp.zeros(grad_s.shape, BF16)
    me = member_ref[0]
    for first in range(0, VARS, 16):
        rows = min(16, VARS - first)
        mine = pred_s[me, first : first + rows, :]
        total = jnp.zeros_like(mine)
        for member in range(MEMBERS):
            total = total + smooth_slope(mine - pred_s[member, first : first + rows, :])
        slopes = smooth_slope(mine - target_ref[first : first + rows, :]) - total * (
            1.0 / (MEMBERS - 1)
        )
        grad_s[first : first + rows, :] = (weight_ref[first : first + rows, :] * slopes).astype(
            BF16
        )
    grads = grad_s[...]
    sums = dot(mix, grads, NT)
    to_far_ref[...] = sums[0:NODES]
    own_ref[...] = sums[NODES : 2 * NODES]
    to_mate_ref[...] = sums[2 * NODES : SPAN]
    turned = dot(grads, mix, NT).astype(BF16)
    bands = (far_states_ref.ready(), states_ref.ready().at[0], mate_states_ref.ready())
    for block in range(WIDTH // NODES):
        cols = slice(block * NODES, (block + 1) * NODES)
        states = jnp.concatenate([band[:, cols] for band in bands], axis=0)
        dec = jnp.transpose(dot(turned, states, NN)).astype(BF16)
        count = NODES // DEC_ROWS
        terms_ref[block * count : (block + 1) * count, 0:DEC_ROWS, :] = dec.reshape(
            count, DEC_ROWS, VARS_LANE
        )
    attn_ref = attn_ref.ready()
    source = lax.broadcasted_iota(jnp.int32, (PAIR, PAIR), 1)
    place = ((source & 6) << 4) + ((source & 8) << 1) + ((source & 112) >> 3) + (source & 1)
    order = (lax.broadcasted_iota(jnp.int32, (PAIR, PAIR), 0) == place).astype(BF16)
    for block in range(ATT // PAIR):
        first = MEMBERS * VARS_SUB + block * NODES
        rows = slice(first, first + NODES)
        attn = jnp.concatenate([far_ref[rows], attn_ref[block], mate_ref[rows]], axis=0)
        wo = dot(order, dot(turned, attn, NN).astype(BF16), NT).astype(BF16)
        for part in range(NODES // WO_ROWS):
            row, core = part // 2, part % 2
            terms_ref[(row * 4 + block) * 2 + core, DEC_ROWS:ROWS, :] = wo[
                part * WO_ROWS : (part + 1) * WO_ROWS
            ]


def total_of(in_ref):
    total = in_ref[0].astype(F32)
    for i in range(1, in_ref.shape[0]):
        total = total + in_ref[i].astype(F32)
    return total


def near_body(in_ref, out_ref):
    total = total_of(in_ref)
    dec = total[0:DEC_ROWS]
    rest = jnp.zeros((SENT - DEC_ROWS - OWN_ROWS, VARS_LANE), F32)
    for i in range(FAR_SIZE):
        first = DEC_ROWS + OWN_ROWS * (i % 8)
        sent = jnp.concatenate([dec, total[first : first + OWN_ROWS], rest], axis=0)
        out_ref[i] = sent.astype(BF16)


def sum_body(in_ref, out_ref):
    total = total_of(in_ref).astype(BF16)
    for i in range(NEAR_SIZE):
        out_ref[i] = total


def final_body(band_ref, all_ref, dec_ref, after_ref, wo_ref, grad_dec_ref, dec_s):
    dec_s[...] = jnp.zeros(dec_s.shape, BF16)
    dec_s[0:VARS, :] = dec_ref[...]
    column, core = lax.div(band_ref[0], 16), lax.rem(band_ref[0], 2)
    rows = [
        all_ref[(row * 4 + column) * 2 + core].astype(F32)[DEC_ROWS : DEC_ROWS + OWN_ROWS]
        for row in range(4)
    ]
    wo_ref[...] = dot(jnp.concatenate(rows, axis=0).astype(BF16), dec_s[...], NN)
    dec = all_ref[:, 0:DEC_ROWS, :].astype(F32).reshape(WIDTH, VARS_LANE)
    grad_dec_ref[...] = jnp.transpose(dec)[0:VARS, :]


def pair_masks(dtype):
    lane = lax.broadcasted_iota(jnp.int32, (1, PAIR), 1)
    return (lane < HEAD_DIM).astype(dtype), (lane >= HEAD_DIM).astype(dtype)


def band_blocks(far_ref, own_ref, mate_ref, pair, first):
    cols = slice(pair * PAIR, (pair + 1) * PAIR)
    side = slice(first + pair * PAIR, first + (pair + 1) * PAIR)
    return jnp.concatenate([far_ref[:, side], own_ref[0, :, cols], mate_ref[:, side]], axis=0)


def probabilities(inside, query_ref, key_ref, mate_ref, far_ref, pair):
    masks = pair_masks(BF16)
    query = query_ref[0, :, pair * PAIR : (pair + 1) * PAIR]
    keys = band_blocks(far_ref, key_ref, mate_ref, pair, 0)
    probs = []
    for half in range(2):
        scores = dot(query * masks[half], keys, NT) * SCALE
        scores = jnp.where(inside, scores, MASKED_SCORE)
        exponent = jnp.exp(scores - jnp.max(scores, axis=-1, keepdims=True))
        probs.append(exponent / jnp.sum(exponent, axis=-1, keepdims=True))
    return probs


def window(band_ref, windows_ref):
    lanes = lax.broadcasted_iota(jnp.int32, (1, NODES), 1)
    place = jnp.concatenate([lanes + base for base in bases(band_ref[0])], axis=1)
    return (place >= windows_ref[0, 0]) & (place < windows_ref[1, 0])


def forward_body(
    band_ref, windows_ref, query_ref, key_ref, value_ref, mate_ref, far_ref, attn_ref
):
    query_ref, key_ref, value_ref = query_ref.ready(), key_ref.ready(), value_ref.ready()
    far_ref, mate_ref = far_ref.ready(), mate_ref.ready()
    inside = window(band_ref, windows_ref)
    lane = lax.broadcasted_iota(jnp.int32, (1, PAIR), 1)
    for pair in range(HEADS // 2):
        values = band_blocks(far_ref, value_ref, mate_ref, pair, ATT)
        outs = [
            dot(prob.astype(BF16), values, NN)
            for prob in probabilities(inside, query_ref, key_ref, mate_ref, far_ref, pair)
        ]
        attn_ref[pair] = jnp.where(lane < HEAD_DIM, outs[0], outs[1]).astype(BF16)


def prob_body(
    band_ref, windows_ref, query_ref, key_ref, mate_ref, far_ref, after_ref, prob_ref, done_ref
):
    done_ref[...] = jnp.zeros(done_ref.shape, F32)
    query_ref, key_ref = query_ref.ready(), key_ref.ready()
    far_ref, mate_ref = far_ref.ready(), mate_ref.ready()
    inside = window(band_ref, windows_ref)
    for pair in range(HEADS // 2):
        probs = probabilities(inside, query_ref, key_ref, mate_ref, far_ref, pair)
        prob_ref[2 * pair] = probs[0]
        prob_ref[2 * pair + 1] = probs[1]


def backward_body(
    own_sum_ref,
    far_sum_ref,
    mate_sum_ref,
    dec_ref,
    out_weight_ref,
    query_ref,
    key_ref,
    value_ref,
    far_ref,
    mate_ref,
    prob_ref,
    after_ref,
    states_ref,
    grad_query_ref,
    to_far_ref,
    own_ref,
    to_mate_ref,
    dec_s,
):
    dec_s[...] = jnp.zeros(dec_s.shape, BF16)
    dec_s[0:VARS, :] = dec_ref.ready()[...]
    dec = dec_s[...]
    total = own_sum_ref.ready()[...] + far_sum_ref.ready()[...] + mate_sum_ref.ready()[...]
    grad_states = dot(
        jnp.concatenate(split(total), axis=1), jnp.concatenate([dec, dec], axis=0), NN
    ).astype(BF16)
    states_ref[0] = grad_states
    grad_out = dot(grad_states, out_weight_ref.ready()[...], NT).astype(BF16)
    query_ref, key_ref, value_ref = query_ref.ready(), key_ref.ready(), value_ref.ready()
    far_ref, mate_ref, prob_ref = far_ref.ready(), mate_ref.ready(), prob_ref.ready()
    masks = pair_masks(BF16)
    lane = lax.broadcasted_iota(jnp.int32, (1, PAIR), 1)
    first = lane < HEAD_DIM
    for pair in range(HEADS // 2):
        cols = slice(pair * PAIR, (pair + 1) * PAIR)
        vcols = slice(ATT + pair * PAIR, ATT + (pair + 1) * PAIR)
        query = query_ref[0, :, cols]
        keys = band_blocks(far_ref, key_ref, mate_ref, pair, 0)
        values = band_blocks(far_ref, value_ref, mate_ref, pair, ATT)
        grads = grad_out[:, cols]
        key_terms, value_terms, query_terms = [], [], []
        for half in range(2):
            prob = prob_ref[2 * pair + half]
            grad_prob = dot(grads * masks[half], values, NT)
            delta = jnp.sum(prob * grad_prob, axis=-1, keepdims=True)
            grad_scores = (prob * (grad_prob - delta)).astype(BF16)
            value_terms.append(dot(prob.astype(BF16), grads, TN))
            query_terms.append(dot(grad_scores, keys, NN))
            key_terms.append(dot(grad_scores, query, TN))
        grad_query_ref[0, :, cols] = (
            jnp.where(first, query_terms[0], query_terms[1]) * SCALE
        ).astype(BF16)
        key_term = jnp.where(first, key_terms[0], key_terms[1]) * SCALE
        value_term = jnp.where(first, value_terms[0], value_terms[1])
        for term, where in ((key_term, cols), (value_term, vcols)):
            to_far_ref[:, where] = term[0:NODES].astype(BF16)
            own_ref[:, where] = term[NODES : 2 * NODES]
            to_mate_ref[:, where] = term[2 * NODES : SPAN].astype(BF16)


def join_body(own_ref, far_ref, mate_ref, key_ref, value_ref, done_ref):
    done_ref[...] = jnp.zeros(done_ref.shape, F32)
    own_ref, far_ref, mate_ref = own_ref.ready(), far_ref.ready(), mate_ref.ready()
    for first, ref in ((0, key_ref), (ATT, value_ref)):
        cols = slice(first, first + ATT)
        ref[0] = (
            own_ref[:, cols] + far_ref[:, cols].astype(F32) + mate_ref[:, cols].astype(F32)
        ).astype(BF16)


def swap_far(x):
    pairs = [(i, i + 1) for i in range(1, 63, 2)]
    return lax.ppermute(x, SPACE, pairs + [(target, source) for source, target in pairs])


def swap_mate(x):
    return lax.ppermute(x, "c", [(0, 1), (1, 0)])


def exchange(x, axes):
    return lax.all_to_all(x, axes, split_axis=0, concat_axis=0, tiled=True)


def per_device(
    node_states,
    query,
    key,
    value,
    out_weight,
    dec_weight,
    target,
    area_weight,
    var_weight,
    edges,
    edge_weight,
    windows,
):
    band = lax.axis_index(SPACE).astype(jnp.int32).reshape(1)
    member = (2 * lax.axis_index("y")).astype(jnp.int32).reshape(1)
    proj = call(
        project_body,
        shape((VARS_SUB, NODES), BF16),
        "ll",
        (node_states, dec_weight),
        scratch=[pltpu.VMEM((VARS_SUB, WIDTH), BF16)],
        limit=WHOLE,
    )
    other = lax.ppermute(proj, "zh", [(0, 1), (1, 0)])
    packed = call(
        pack_body,
        shape((NODES, 2 * WIDTH), BF16),
        "aaaa",
        (node_states, key, value, proj),
        scratch=[pltpu.SemaphoreType.DMA((3,))],
        limit=WHOLE,
    )
    mate_band, far_band = swap_mate(packed), swap_far(packed)
    pairs = call(
        pair_body,
        shape((4, 2 * VARS_SUB, NODES), BF16),
        "ll",
        (proj, other),
        cost=LONG,
    )
    mid = exchange(pairs, "y")
    attn = call(
        forward_body,
        shape((ATT // PAIR, NODES, PAIR), BF16),
        "sslllkk",
        (band, windows, query, key, value, mate_band, far_band),
    )
    mix, weight = call(
        weights_body,
        (shape((SPAN, POINTS), BF16), shape((VARS_SUB, POINTS), F32)),
        "svvvv",
        (band, edges, edge_weight, area_weight.reshape(1, -1), var_weight.reshape(1, -1)),
    )
    halo = jnp.concatenate([mid.reshape(-1, NODES), attn.reshape(-1, PAIR)], axis=0)
    mate_halo, far_halo = swap_mate(halo), swap_far(halo)
    flag = shape((8, 128), F32)
    prob, done = call(
        prob_body,
        (shape((HEADS, NODES, SPAN), F32), flag),
        "ssllkka",
        (band, windows, query, key, mate_band, far_band, halo),
        cost=LONG,
    )
    block = shape((NODES, VARS_LANE), F32)
    terms, to_far, own, to_mate = call(
        crps_body,
        (shape((NEAR_SIZE, ROWS, VARS_LANE), BF16), block, block, block),
        "svvvvvvllttv",
        (
            member,
            mate_halo,
            mid,
            far_halo,
            mix,
            weight,
            target,
            attn,
            node_states,
            mate_band,
            far_band,
            done,
        ),
        scratch=[
            pltpu.VMEM((MEMBERS, VARS_SUB, POINTS), F32),
            pltpu.VMEM((VARS_LANE, POINTS), BF16),
        ],
    )
    near = exchange(terms, NEAR)
    mate_sum, far_sum = swap_mate(to_mate), swap_far(to_far)
    near_sums = call(
        near_body, shape((FAR_SIZE, SENT, VARS_LANE), BF16), "v", (near,), cost=LONG
    )
    along = exchange(near_sums, FAR)
    wide = (NODES, 2 * ATT)
    grad_states, grad_query, kv_far, kv_own, kv_mate = call(
        backward_body,
        (
            shape((1, NODES, WIDTH), BF16),
            shape((1, NODES, ATT), BF16),
            shape(wide, BF16),
            shape(wide, F32),
            shape(wide, BF16),
        ),
        "llllllllkkla",
        (
            own,
            far_sum,
            mate_sum,
            dec_weight,
            out_weight,
            query,
            key,
            value,
            far_band,
            mate_band,
            prob,
            near_sums,
        ),
        scratch=[pltpu.VMEM((VARS_LANE, WIDTH), BF16)],
        limit=WHOLE,
        cost=LONG,
    )
    far_sums = call(
        sum_body,
        shape((NEAR_SIZE, SENT, VARS_LANE), BF16),
        "v",
        (along,),
        cost=LONG,
    )
    everything = exchange(far_sums, NEAR)
    mate_term, far_term = swap_mate(kv_mate), swap_far(kv_far)
    grad_key, grad_value, joined = call(
        join_body,
        (shape((1, NODES, ATT), BF16), shape((1, NODES, ATT), BF16), flag),
        "lll",
        (kv_own, far_term, mate_term),
        cost=LONG,
    )
    grad_wo, grad_dec = call(
        final_body,
        (shape((8, WIDTH), F32), shape((VARS, WIDTH), F32)),
        "svva",
        (band, everything, dec_weight, joined),
        scratch=[pltpu.VMEM((VARS_LANE, WIDTH), BF16)],
    )
    return grad_states, grad_query, grad_key, grad_value, grad_wo, grad_dec


def solution(mesh):
    fine = Mesh(mesh.devices.reshape(SIZES), AXES)
    in_specs = (
        P(ENS, SPACE, None),
        P(ENS, SPACE, None),
        P(ENS, SPACE, None),
        P(ENS, SPACE, None),
        P(),
        P(),
        P(None, SPACE),
        P(SPACE),
        P(),
        P(None, SPACE),
        P(None, SPACE),
        P(None, SPACE),
    )
    out_specs = (
        P(ENS, SPACE, None),
        P(ENS, SPACE, None),
        P(ENS, SPACE, None),
        P(ENS, SPACE, None),
        P(SPACE, None),
        P(),
    )
    return jax.shard_map(
        per_device, mesh=fine, in_specs=in_specs, out_specs=out_specs, check_vma=False
    )
```

```python
import math

import jax
import jax.numpy as jnp
from jax import lax
from jax.experimental import pallas as pl
from jax.experimental.pallas import tpu as pltpu
from jax.sharding import Mesh
from jax.sharding import PartitionSpec as P

HEADS = 8
HEAD_DIM = 64
PAIR = 2 * HEAD_DIM
VARS = 100
VARS_SUB = 112
VARS_LANE = 128
MEMBERS = 8
NODES = 128
POINTS = 1024
SPAN = 3 * NODES
WIDTH = 1024
ATT = 512
SMOOTH_SQUARE = 0.0625
MASKED_SCORE = -1e30
SCALE = 1.0 / math.sqrt(HEAD_DIM)

AXES = ("zh", "y", "x", "zl", "c")
SIZES = (2, 4, 4, 8, 2)
ENS = ("zh", "y")
SPACE = ("x", "zl", "c")
NEAR = ("y", "x", "c")
NEAR_SIZE = 32
FAR = ("zh", "zl")
FAR_SIZE = 16
DEC_ROWS = WIDTH // NEAR_SIZE
WO_ROWS = ATT // NEAR_SIZE
ROWS = DEC_ROWS + WO_ROWS
OWN_ROWS = 2
SENT = DEC_ROWS + 8

WHOLE = 58 * 2**20
LONG = 2 * 10**10

F32 = jnp.float32
BF16 = jnp.bfloat16
NN = (((1,), (0,)), ((), ()))
NT = (((1,), (1,)), ((), ()))
TN = (((0,), (0,)), ((), ()))


def dot(a, b, dims):
    return lax.dot_general(a, b, dims, preferred_element_type=F32)


class Landing:
    def __init__(self, source, target, sem):
        self.target = target
        self.copy = pltpu.make_async_copy(source, target, sem)
        self.copy.start()

    def ready(self):
        self.copy.wait()
        return self.target


def call(body, out_shape, spaces, args, scratch=(), cost=10**8, limit=24 * 2**20):
    kinds = {
        "s": pl.BlockSpec(memory_space=pltpu.SMEM),
        "v": pl.BlockSpec(memory_space=pltpu.VMEM),
    }
    left = pl.BlockSpec(memory_space=pl.ANY)
    specs = [kinds.get(space, left) for space in spaces]
    landed = [i for i, space in enumerate(spaces) if space in "ltk"]
    outs = len(out_shape) if isinstance(out_shape, tuple) else 1
    if landed:
        targets = [
            pltpu.VMEM(args[i].shape if spaces[i] == "l" else (NODES, WIDTH), args[i].dtype)
            for i in landed
        ]
        scratch = [*targets, pltpu.SemaphoreType.DMA((len(landed),)), *scratch]

    def kernel(*refs):
        inputs = list(refs[: len(args)])
        results = refs[len(args) : len(args) + outs]
        rest = refs[len(args) + outs :]
        if landed:
            count = len(landed)
            for k, i in enumerate(landed):
                source = inputs[i]
                if spaces[i] == "t":
                    source = source.at[:, pl.ds(0, WIDTH)]
                if spaces[i] == "k":
                    source = source.at[:, pl.ds(WIDTH, WIDTH)]
                inputs[i] = Landing(source, rest[k], rest[count].at[k])
            rest = rest[count + 1 :]
        body(*inputs, *results, *rest)

    return pl.pallas_call(
        kernel,
        out_shape=out_shape,
        in_specs=specs,
        scratch_shapes=list(scratch),
        compiler_params=pltpu.CompilerParams(vmem_limit_bytes=limit),
        cost_estimate=pl.CostEstimate(flops=cost, bytes_accessed=10**6, transcendentals=0),
    )(*args)


def shape(dims, dtype):
    return jax.ShapeDtypeStruct(dims, dtype)


def smooth_slope(t):
    return t * lax.rsqrt(t * t + SMOOTH_SQUARE)


def split(x):
    high = x.astype(BF16)
    return high, (x - high.astype(F32)).astype(BF16)


def project_body(states_ref, dec_ref, proj_ref, pad_s):
    pad_s[...] = jnp.zeros(pad_s.shape, BF16)
    pad_s[0:VARS, :] = dec_ref.ready()[...]
    proj_ref[...] = dot(pad_s[...], states_ref.ready()[0], NT).astype(BF16)


def pack_body(states_hbm, key_hbm, value_hbm, after_ref, out_ref, sems):
    copies = [
        pltpu.make_async_copy(states_hbm.at[0], out_ref.at[:, pl.ds(0, WIDTH)], sems.at[0]),
        pltpu.make_async_copy(key_hbm.at[0], out_ref.at[:, pl.ds(WIDTH, ATT)], sems.at[1]),
        pltpu.make_async_copy(value_hbm.at[0], out_ref.at[:, pl.ds(WIDTH + ATT, ATT)], sems.at[2]),
    ]
    for copy in copies:
        copy.start()
    for copy in copies:
        copy.wait()


def pair_body(own_ref, other_ref, out_ref):
    own_ref, other_ref = own_ref.ready(), other_ref.ready()
    for i in range(out_ref.shape[0]):
        out_ref[i, 0:VARS_SUB, :] = own_ref[...]
        out_ref[i, VARS_SUB : 2 * VARS_SUB, :] = other_ref[...]


def bases(band):
    side = 2 * lax.rem(band, 2) - 1
    return (band + side) * NODES, band * NODES, (band - side) * NODES


def weights_body(band_ref, edges_ref, edge_weight_ref, area_ref, var_ref, mix_ref, weight_ref):
    edges = edges_ref[...]
    for part, base in enumerate(bases(band_ref[0])):
        place = lax.broadcasted_iota(jnp.int32, (NODES, POINTS), 0) + base
        mix = jnp.zeros((NODES, POINTS), F32)
        for slot in range(3):
            mix = mix + jnp.where(
                edges[slot : slot + 1, :] == place, edge_weight_ref[slot : slot + 1, :], 0.0
            )
        mix_ref[part * NODES : (part + 1) * NODES, :] = mix.astype(BF16)
    row = jnp.concatenate([var_ref[...], jnp.zeros((1, VARS_LANE - VARS), F32)], axis=1)
    column = jnp.transpose(jnp.broadcast_to(row, (VARS_LANE, VARS_LANE)))[0:VARS_SUB, 0:1]
    weight_ref[...] = column * area_ref[...]


def crps_body(
    member_ref,
    mate_ref,
    mid_ref,
    far_ref,
    mix_ref,
    weight_ref,
    target_ref,
    attn_ref,
    states_ref,
    mate_states_ref,
    far_states_ref,
    after_ref,
    terms_ref,
    to_far_ref,
    own_ref,
    to_mate_ref,
    pred_s,
    grad_s,
):
    mix = mix_ref[...]
    for member in range(MEMBERS):
        rows = slice(member * VARS_SUB, (member + 1) * VARS_SUB)
        half = slice((member % 2) * VARS_SUB, (member % 2 + 1) * VARS_SUB)
        proj = jnp.concatenate([far_ref[rows], mid_ref[member // 2, half], mate_ref[rows]], axis=1)
        pred_s[member] = dot(proj, mix, NN)
    grad_s[...] = jnp.zeros(grad_s.shape, BF16)
    me = member_ref[0]
    for first in range(0, VARS, 16):
        rows = min(16, VARS - first)
        mine = pred_s[me, first : first + rows, :]
        total = jnp.zeros_like(mine)
        for member in range(MEMBERS):
            total = total + smooth_slope(mine - pred_s[member, first : first + rows, :])
        slopes = smooth_slope(mine - target_ref[first : first + rows, :]) - total * (
            1.0 / (MEMBERS - 1)
        )
        grad_s[first : first + rows, :] = (weight_ref[first : first + rows, :] * slopes).astype(
            BF16
        )
    grads = grad_s[...]
    sums = dot(mix, grads, NT)
    to_far_ref[...] = sums[0:NODES]
    own_ref[...] = sums[NODES : 2 * NODES]
    to_mate_ref[...] = sums[2 * NODES : SPAN]
    turned = dot(grads, mix, NT).astype(BF16)
    bands = (far_states_ref.ready(), states_ref.ready().at[0], mate_states_ref.ready())
    for block in range(WIDTH // NODES):
        cols = slice(block * NODES, (block + 1) * NODES)
        states = jnp.concatenate([band[:, cols] for band in bands], axis=0)
        dec = jnp.transpose(dot(turned, states, NN)).astype(BF16)
        count = NODES // DEC_ROWS
        terms_ref[block * count : (block + 1) * count, 0:DEC_ROWS, :] = dec.reshape(
            count, DEC_ROWS, VARS_LANE
        )
    attn_ref = attn_ref.ready()
    source = lax.broadcasted_iota(jnp.int32, (PAIR, PAIR), 1)
    place = ((source & 6) << 4) + ((source & 8) << 1) + ((source & 112) >> 3) + (source & 1)
    order = (lax.broadcasted_iota(jnp.int32, (PAIR, PAIR), 0) == place).astype(BF16)
    for block in range(ATT // PAIR):
        first = MEMBERS * VARS_SUB + block * NODES
        rows = slice(first, first + NODES)
        attn = jnp.concatenate([far_ref[rows], attn_ref[block], mate_ref[rows]], axis=0)
        wo = dot(order, dot(turned, attn, NN).astype(BF16), NT).astype(BF16)
        for part in range(NODES // WO_ROWS):
            row, core = part // 2, part % 2
            terms_ref[(row * 4 + block) * 2 + core, DEC_ROWS:ROWS, :] = wo[
                part * WO_ROWS : (part + 1) * WO_ROWS
            ]


def total_of(in_ref):
    total = in_ref[0].astype(F32)
    for i in range(1, in_ref.shape[0]):
        total = total + in_ref[i].astype(F32)
    return total


def near_body(in_ref, out_ref):
    total = total_of(in_ref)
    dec = total[0:DEC_ROWS]
    rest = jnp.zeros((SENT - DEC_ROWS - OWN_ROWS, VARS_LANE), F32)
    for i in range(FAR_SIZE):
        first = DEC_ROWS + OWN_ROWS * (i % 8)
        sent = jnp.concatenate([dec, total[first : first + OWN_ROWS], rest], axis=0)
        out_ref[i] = sent.astype(BF16)


def sum_body(in_ref, after_ref, out_ref):
    total = total_of(in_ref).astype(BF16)
    for i in range(NEAR_SIZE):
        out_ref[i] = total


def final_body(band_ref, all_ref, dec_ref, after_ref, wo_ref, grad_dec_ref, dec_s):
    dec_s[...] = jnp.zeros(dec_s.shape, BF16)
    dec_s[0:VARS, :] = dec_ref[...]
    column, core = lax.div(band_ref[0], 16), lax.rem(band_ref[0], 2)
    rows = [
        all_ref[(row * 4 + column) * 2 + core].astype(F32)[DEC_ROWS : DEC_ROWS + OWN_ROWS]
        for row in range(4)
    ]
    wo_ref[...] = dot(jnp.concatenate(rows, axis=0).astype(BF16), dec_s[...], NN)
    dec = all_ref[:, 0:DEC_ROWS, :].astype(F32).reshape(WIDTH, VARS_LANE)
    grad_dec_ref[...] = jnp.transpose(dec)[0:VARS, :]


def pair_masks(dtype):
    lane = lax.broadcasted_iota(jnp.int32, (1, PAIR), 1)
    return (lane < HEAD_DIM).astype(dtype), (lane >= HEAD_DIM).astype(dtype)


def band_blocks(far_ref, own_ref, mate_ref, pair, first):
    cols = slice(pair * PAIR, (pair + 1) * PAIR)
    side = slice(first + pair * PAIR, first + (pair + 1) * PAIR)
    return jnp.concatenate([far_ref[:, side], own_ref[0, :, cols], mate_ref[:, side]], axis=0)


def probabilities(inside, query_ref, key_ref, mate_ref, far_ref, pair):
    masks = pair_masks(BF16)
    query = query_ref[0, :, pair * PAIR : (pair + 1) * PAIR]
    keys = band_blocks(far_ref, key_ref, mate_ref, pair, 0)
    probs = []
    for half in range(2):
        scores = dot(query * masks[half], keys, NT) * SCALE
        scores = jnp.where(inside, scores, MASKED_SCORE)
        exponent = jnp.exp(scores - jnp.max(scores, axis=-1, keepdims=True))
        probs.append(exponent / jnp.sum(exponent, axis=-1, keepdims=True))
    return probs


def window(band_ref, windows_ref):
    lanes = lax.broadcasted_iota(jnp.int32, (1, NODES), 1)
    place = jnp.concatenate([lanes + base for base in bases(band_ref[0])], axis=1)
    return (place >= windows_ref[0, 0]) & (place < windows_ref[1, 0])


def forward_body(
    band_ref, windows_ref, query_ref, key_ref, value_ref, mate_ref, far_ref, attn_ref
):
    query_ref, key_ref, value_ref = query_ref.ready(), key_ref.ready(), value_ref.ready()
    far_ref, mate_ref = far_ref.ready(), mate_ref.ready()
    inside = window(band_ref, windows_ref)
    lane = lax.broadcasted_iota(jnp.int32, (1, PAIR), 1)
    for pair in range(HEADS // 2):
        values = band_blocks(far_ref, value_ref, mate_ref, pair, ATT)
        outs = [
            dot(prob.astype(BF16), values, NN)
            for prob in probabilities(inside, query_ref, key_ref, mate_ref, far_ref, pair)
        ]
        attn_ref[pair] = jnp.where(lane < HEAD_DIM, outs[0], outs[1]).astype(BF16)


def prob_body(
    band_ref, windows_ref, query_ref, key_ref, mate_ref, far_ref, after_ref, prob_ref, done_ref
):
    done_ref[...] = jnp.zeros(done_ref.shape, F32)
    query_ref, key_ref = query_ref.ready(), key_ref.ready()
    far_ref, mate_ref = far_ref.ready(), mate_ref.ready()
    inside = window(band_ref, windows_ref)
    for pair in range(HEADS // 2):
        probs = probabilities(inside, query_ref, key_ref, mate_ref, far_ref, pair)
        prob_ref[2 * pair] = probs[0]
        prob_ref[2 * pair + 1] = probs[1]


def backward_body(
    own_sum_ref,
    far_sum_ref,
    mate_sum_ref,
    dec_ref,
    out_weight_ref,
    query_ref,
    key_ref,
    value_ref,
    far_ref,
    mate_ref,
    prob_ref,
    after_ref,
    states_ref,
    grad_query_ref,
    to_far_ref,
    own_ref,
    to_mate_ref,
    dec_s,
):
    dec_s[...] = jnp.zeros(dec_s.shape, BF16)
    dec_s[0:VARS, :] = dec_ref.ready()[...]
    dec = dec_s[...]
    total = own_sum_ref.ready()[...] + far_sum_ref.ready()[...] + mate_sum_ref.ready()[...]
    grad_states = dot(
        jnp.concatenate(split(total), axis=1), jnp.concatenate([dec, dec], axis=0), NN
    ).astype(BF16)
    states_ref[0] = grad_states
    grad_out = dot(grad_states, out_weight_ref.ready()[...], NT).astype(BF16)
    query_ref, key_ref, value_ref = query_ref.ready(), key_ref.ready(), value_ref.ready()
    far_ref, mate_ref, prob_ref = far_ref.ready(), mate_ref.ready(), prob_ref.ready()
    masks = pair_masks(BF16)
    lane = lax.broadcasted_iota(jnp.int32, (1, PAIR), 1)
    first = lane < HEAD_DIM
    for pair in range(HEADS // 2):
        cols = slice(pair * PAIR, (pair + 1) * PAIR)
        vcols = slice(ATT + pair * PAIR, ATT + (pair + 1) * PAIR)
        query = query_ref[0, :, cols]
        keys = band_blocks(far_ref, key_ref, mate_ref, pair, 0)
        values = band_blocks(far_ref, value_ref, mate_ref, pair, ATT)
        grads = grad_out[:, cols]
        key_terms, value_terms, query_terms = [], [], []
        for half in range(2):
            prob = prob_ref[2 * pair + half]
            grad_prob = dot(grads * masks[half], values, NT)
            delta = jnp.sum(prob * grad_prob, axis=-1, keepdims=True)
            grad_scores = (prob * (grad_prob - delta)).astype(BF16)
            value_terms.append(dot(prob.astype(BF16), grads, TN))
            query_terms.append(dot(grad_scores, keys, NN))
            key_terms.append(dot(grad_scores, query, TN))
        grad_query_ref[0, :, cols] = (
            jnp.where(first, query_terms[0], query_terms[1]) * SCALE
        ).astype(BF16)
        key_term = jnp.where(first, key_terms[0], key_terms[1]) * SCALE
        value_term = jnp.where(first, value_terms[0], value_terms[1])
        for term, where in ((key_term, cols), (value_term, vcols)):
            to_far_ref[:, where] = term[0:NODES].astype(BF16)
            own_ref[:, where] = term[NODES : 2 * NODES]
            to_mate_ref[:, where] = term[2 * NODES : SPAN].astype(BF16)


def join_body(own_ref, far_ref, mate_ref, key_ref, value_ref, done_ref):
    done_ref[...] = jnp.zeros(done_ref.shape, F32)
    own_ref, far_ref, mate_ref = own_ref.ready(), far_ref.ready(), mate_ref.ready()
    for first, ref in ((0, key_ref), (ATT, value_ref)):
        cols = slice(first, first + ATT)
        ref[0] = (
            own_ref[:, cols] + far_ref[:, cols].astype(F32) + mate_ref[:, cols].astype(F32)
        ).astype(BF16)


def swap_far(x):
    pairs = [(i, i + 1) for i in range(1, 63, 2)]
    return lax.ppermute(x, SPACE, pairs + [(target, source) for source, target in pairs])


def swap_mate(x):
    return lax.ppermute(x, "c", [(0, 1), (1, 0)])


def exchange(x, axes):
    return lax.all_to_all(x, axes, split_axis=0, concat_axis=0, tiled=True)


def per_device(
    node_states,
    query,
    key,
    value,
    out_weight,
    dec_weight,
    target,
    area_weight,
    var_weight,
    edges,
    edge_weight,
    windows,
):
    band = lax.axis_index(SPACE).astype(jnp.int32).reshape(1)
    member = (2 * lax.axis_index("y")).astype(jnp.int32).reshape(1)
    proj = call(
        project_body,
        shape((VARS_SUB, NODES), BF16),
        "ll",
        (node_states, dec_weight),
        scratch=[pltpu.VMEM((VARS_SUB, WIDTH), BF16)],
        limit=WHOLE,
    )
    other = lax.ppermute(proj, "zh", [(0, 1), (1, 0)])
    packed = call(
        pack_body,
        shape((NODES, 2 * WIDTH), BF16),
        "aaaa",
        (node_states, key, value, proj),
        scratch=[pltpu.SemaphoreType.DMA((3,))],
        limit=WHOLE,
    )
    mate_band, far_band = swap_mate(packed), swap_far(packed)
    pairs = call(
        pair_body,
        shape((4, 2 * VARS_SUB, NODES), BF16),
        "ll",
        (proj, other),
        cost=LONG,
    )
    mid = exchange(pairs, "y")
    attn = call(
        forward_body,
        shape((ATT // PAIR, NODES, PAIR), BF16),
        "sslllkk",
        (band, windows, query, key, value, mate_band, far_band),
    )
    mix, weight = call(
        weights_body,
        (shape((SPAN, POINTS), BF16), shape((VARS_SUB, POINTS), F32)),
        "svvvv",
        (band, edges, edge_weight, area_weight.reshape(1, -1), var_weight.reshape(1, -1)),
    )
    halo = jnp.concatenate([mid.reshape(-1, NODES), attn.reshape(-1, PAIR)], axis=0)
    mate_halo, far_halo = swap_mate(halo), swap_far(halo)
    flag = shape((8, 128), F32)
    prob, done = call(
        prob_body,
        (shape((HEADS, NODES, SPAN), F32), flag),
        "ssllkka",
        (band, windows, query, key, mate_band, far_band, halo),
        cost=LONG,
    )
    block = shape((NODES, VARS_LANE), F32)
    terms, to_far, own, to_mate = call(
        crps_body,
        (shape((NEAR_SIZE, ROWS, VARS_LANE), BF16), block, block, block),
        "svvvvvvllttv",
        (
            member,
            mate_halo,
            mid,
            far_halo,
            mix,
            weight,
            target,
            attn,
            node_states,
            mate_band,
            far_band,
            done,
        ),
        scratch=[
            pltpu.VMEM((MEMBERS, VARS_SUB, POINTS), F32),
            pltpu.VMEM((VARS_LANE, POINTS), BF16),
        ],
    )
    near = exchange(terms, NEAR)
    mate_sum, far_sum = swap_mate(to_mate), swap_far(to_far)
    near_sums = call(
        near_body, shape((FAR_SIZE, SENT, VARS_LANE), BF16), "v", (near,), cost=LONG
    )
    along = exchange(near_sums, FAR)
    wide = (NODES, 2 * ATT)
    grad_states, grad_query, kv_far, kv_own, kv_mate = call(
        backward_body,
        (
            shape((1, NODES, WIDTH), BF16),
            shape((1, NODES, ATT), BF16),
            shape(wide, BF16),
            shape(wide, F32),
            shape(wide, BF16),
        ),
        "llllllllkkla",
        (
            own,
            far_sum,
            mate_sum,
            dec_weight,
            out_weight,
            query,
            key,
            value,
            far_band,
            mate_band,
            prob,
            near_sums,
        ),
        scratch=[pltpu.VMEM((VARS_LANE, WIDTH), BF16)],
        limit=WHOLE,
        cost=LONG,
    )
    far_sums = call(
        sum_body,
        shape((NEAR_SIZE, SENT, VARS_LANE), BF16),
        "va",
        (along, grad_query),
        cost=LONG,
    )
    everything = exchange(far_sums, NEAR)
    mate_term, far_term = swap_mate(kv_mate), swap_far(kv_far)
    grad_key, grad_value, joined = call(
        join_body,
        (shape((1, NODES, ATT), BF16), shape((1, NODES, ATT), BF16), flag),
        "lll",
        (kv_own, far_term, mate_term),
    )
    grad_wo, grad_dec = call(
        final_body,
        (shape((8, WIDTH), F32), shape((VARS, WIDTH), F32)),
        "svva",
        (band, everything, dec_weight, joined),
        scratch=[pltpu.VMEM((VARS_LANE, WIDTH), BF16)],
    )
    return grad_states, grad_query, grad_key, grad_value, grad_wo, grad_dec


def solution(mesh):
    fine = Mesh(mesh.devices.reshape(SIZES), AXES)
    in_specs = (
        P(ENS, SPACE, None),
        P(ENS, SPACE, None),
        P(ENS, SPACE, None),
        P(ENS, SPACE, None),
        P(),
        P(),
        P(None, SPACE),
        P(SPACE),
        P(),
        P(None, SPACE),
        P(None, SPACE),
        P(None, SPACE),
    )
    out_specs = (
        P(ENS, SPACE, None),
        P(ENS, SPACE, None),
        P(ENS, SPACE, None),
        P(ENS, SPACE, None),
        P(SPACE, None),
        P(),
    )
    return jax.shard_map(
        per_device, mesh=fine, in_specs=in_specs, out_specs=out_specs, check_vma=False
    )
```
